32 devices in a mesh: group: 2 (over x), dom: 8 (over z, y), feat: 2 (over core).
Axes of the slice: x: 2, y: 2, z: 4, core: 2. Of those that a mesh axis runs over, the one named last changes fastest.
Arguments:
- grid: bfloat16 [65536, 512], P(('group', 'dom', 'feat')), parts along dimension 0, may hold values from -6 to 6
- mesh_feat: bfloat16 [8192, 512], P(('group', 'dom', 'feat')), parts along dimension 0, may hold values from -6 to 6
- owner: int32 [65536, 1], P(('group', 'dom', 'feat')), parts along dimension 0, may hold values from 0 to 15, as said below
- node: int32 [65536], P(('group', 'dom', 'feat')), parts along dimension 0, may hold values from 0 to 255
- halo_index: int32 [2048], P(('group', 'dom', 'feat')), parts along dimension 0, may hold values from 0 to 255
- edge_src: int32 [8192, 6], P(('group', 'dom', 'feat')), parts along dimension 0, may hold values from 0 to 383
- w_enc1: bfloat16 [512, 512], replicated, may hold values from -0.25 to 0.25
- enc_bias: float32 [512], replicated, may hold values from -4 to 4
- w_enc2: bfloat16 [512, 512], replicated, may hold values from -0.25 to 0.25
- proc_src: bfloat16 [2, 512, 512], replicated, may hold values from -0.25 to 0.25
- proc_dst: bfloat16 [2, 512, 512], replicated, may hold values from -0.25 to 0.25
- proc_bias: float32 [2, 512], replicated, may hold values from -4 to 4
- proc_out: bfloat16 [2, 512, 512], replicated, may hold values from -0.046875 to 0.046875
- dec_grid: bfloat16 [512, 512], replicated, may hold values from -0.25 to 0.25
- dec_mesh: bfloat16 [512, 512], replicated, may hold values from -0.0625 to 0.0625
- dec_out: bfloat16 [512, 512], replicated, may hold values from -0.25 to 0.25
Outputs:
- new_grid: bfloat16 [65536, 512], P(('group', 'dom', 'feat')), parts along dimension 0
The draws below stay inside these ranges and needn't reach their ends.
There are 2 independent parts, one for each index of `group`. The reference program is written for one: setup_inputs(seed, part) draws one part's arguments, and reference() takes and returns one part's arrays. A program takes and returns all parts, laid end to end along the dimension named above; an argument that names none is the same for every part. Nothing has to cross between parts.
Inputs may be any that keep to these rules, and one draw needn't show every extreme that they name: `owner`: the 2048 rows of device p (an aligned block) name partition p or one of the four partitions p-2, p-1, p+1, p+2 (mod 16); each of those four is named at most 256 times by one device's rows, and in every draw some device names one of them exactly 256 times; at least half of a device's rows name p itself.
All inputs are finite; a program needn't handle non-finite values.
Results may differ from the reference program's by a relative error of at most 0.014.
Values may be sent and summed in bfloat16 or wider, within the bound.
No kernel may reach another device: no remote copies, remote signals or barrier semaphores. Data moves between devices by JAX's collectives and lax.ppermute only.
A program may use at most 64 MiB of HBM per device.

```python
import jax
import jax.numpy as jnp

D = 512
G_DEV = 2048
M_DEV = 256
HALO = 64
K = 6
L = 2
NDEV = 16
CAP = 256
GRID = 32768
MESH = 4096
N_DOM = 8
N_FEAT = 2


def draw_owner(key, part):
    key = jax.random.fold_in(key, 11)
    count_key, order_key = jax.random.split(key)
    lowest = max(1, CAP // 4)
    counts = jax.random.randint(count_key, (NDEV, 4), lowest, CAP + 1).astype(jnp.int32)
    counts = counts.at[0, 0].set(CAP)
    bounds = jnp.cumsum(counts, axis=1)
    order_keys = jax.random.split(order_key, NDEV)
    places = jax.vmap(lambda k: jax.random.permutation(k, G_DEV))(order_keys).astype(jnp.int32)
    label = jnp.sum((places[:, :, None] >= bounds[:, None, :]).astype(jnp.int32), axis=-1)
    table = jnp.array([1, 2, -1, -2, 0], jnp.int32)
    steps = table[label]
    owners = (jnp.arange(NDEV, dtype=jnp.int32)[:, None] + steps + NDEV) % NDEV
    return owners.reshape(GRID, 1).astype(jnp.int32)


def plant(values, key, low, largest):
    index_at = [jax.random.randint(jax.random.fold_in(key, axis), (), 0, length) for axis, length in enumerate(values.shape)]
    longest = values.shape.index(max(values.shape))
    beside = index_at[:longest] + [(index_at[longest] + 1) % values.shape[longest]] + index_at[longest + 1:]
    return values.at[tuple(index_at)].set(low).at[tuple(beside)].set(largest)


def levels(rng, shape, pieces, least, high):
    loudness = 1.0
    for dim, blocks in pieces:
        draws = jax.random.uniform(jax.random.fold_in(jax.random.fold_in(rng, 6), dim), (blocks,), jnp.float32, least / len(pieces), high / len(pieces))
        loudness = loudness * jnp.repeat(jnp.exp(draws), shape[dim] // blocks).reshape((-1,) + (1,) * (len(shape) - 1 - dim))
    return loudness


def normal_values(key, shape, width, limit, cuts=(), kind=jnp.bfloat16):
    entries = jax.random.normal(key, shape, jnp.float32) * width
    if len(cuts) > 0:
        entries = levels(key, shape, cuts, -0.22, 0.18) * entries
    return jnp.clip(entries, min=-limit, max=limit).astype(kind)


def setup_inputs(seed: int = 0, part: int = 0) -> dict:
    key_list = jax.random.split(jax.random.key(seed), 17)
    part_splits = jax.random.split(jax.random.fold_in(key_list[16], part), 17)
    return {
        "grid": normal_values(part_splits[0], (GRID, D), 1.0, 6.0, ((0, 16),)),
        "mesh_feat": normal_values(part_splits[1], (MESH, D), 1.0, 6.0, ((0, 16),)),
        "owner": draw_owner(jax.random.fold_in(jax.random.fold_in(key_list[16], part), 71), part),
        "node": plant(jax.random.randint(part_splits[3], (GRID,), 0, M_DEV), jax.random.fold_in(part_splits[3], 1), 0, M_DEV - 1).astype(jnp.int32),
        "halo_index": plant(jax.random.randint(part_splits[4], (NDEV * HALO,), 0, M_DEV), jax.random.fold_in(part_splits[4], 1), 0, M_DEV - 1).astype(jnp.int32),
        "edge_src": plant(jax.random.randint(part_splits[5], (MESH, K), 0, M_DEV + 2 * HALO), jax.random.fold_in(part_splits[5], 1), 0, (M_DEV + 2 * HALO) - 1).astype(jnp.int32),
        "w_enc1": normal_values(key_list[6], (D, D), D ** -0.5, 0.25),
        "enc_bias": normal_values(key_list[7], (D,), 1.0, 4.0, (), jnp.float32),
        "w_enc2": normal_values(key_list[8], (D, D), D ** -0.5, 0.25),
        "proc_src": normal_values(key_list[9], (L, D, D), D ** -0.5, 0.25),
        "proc_dst": normal_values(key_list[10], (L, D, D), D ** -0.5, 0.25),
        "proc_bias": normal_values(key_list[11], (L, D), 1.0, 4.0, (), jnp.float32),
        "proc_out": normal_values(key_list[12], (L, D, D), (K * K * D) ** -0.5, 0.046875),
        "dec_grid": normal_values(key_list[13], (D, D), D ** -0.5, 0.25),
        "dec_mesh": normal_values(key_list[14], (D, D), (16 * D) ** -0.5, 0.0625),
        "dec_out": normal_values(key_list[15], (D, D), D ** -0.5, 0.25),
    }


def reference(grid, mesh_feat, owner, node, halo_index, edge_src, w_enc1, enc_bias, w_enc2, proc_src, proc_dst, proc_bias, proc_out, dec_grid, dec_mesh, dec_out):
    ndev = N_DOM * N_FEAT
    hidden_enc = jax.nn.silu(jnp.dot(grid, w_enc1, preferred_element_type=jnp.float32) + enc_bias).astype(jnp.bfloat16)
    message = jnp.dot(hidden_enc, w_enc2, preferred_element_type=jnp.float32).astype(jnp.bfloat16)
    dest = (owner[:, 0] * M_DEV + node).astype(jnp.int32)
    summed = jax.ops.segment_sum(message.astype(jnp.float32), dest, num_segments=M_DEV * ndev)
    latent = (mesh_feat.astype(jnp.float32) + summed).astype(jnp.bfloat16)
    offsets = (jnp.arange(ndev, dtype=jnp.int32) * M_DEV)[:, None]
    bound_rows = halo_index.reshape(ndev, HALO).astype(jnp.int32) + offsets
    sources = edge_src.reshape(ndev, M_DEV, K)
    for layer in range(L):
        blocks = latent.reshape(ndev, M_DEV, D)
        border = latent[bound_rows]
        extended = jnp.concatenate([blocks, jnp.roll(border, 1, axis=0), jnp.roll(border, -1, axis=0)], axis=1)
        source_proj = jnp.dot(extended.reshape(-1, D), proc_src[layer], preferred_element_type=jnp.float32)
        source_proj = source_proj.reshape(ndev, M_DEV + 2 * HALO, D)
        node_proj = jnp.dot(latent, proc_dst[layer], preferred_element_type=jnp.float32) + proc_bias[layer]
        picked = jax.vmap(lambda table, index: table[index])(source_proj, sources)
        edge_msg = jax.nn.silu(picked + node_proj.reshape(ndev, M_DEV, 1, D)).astype(jnp.bfloat16)
        edge_sum = jnp.sum(edge_msg.astype(jnp.float32), axis=2).astype(jnp.bfloat16).reshape(-1, D)
        latent = (latent.astype(jnp.float32) + jnp.dot(edge_sum, proc_out[layer], preferred_element_type=jnp.float32)).astype(jnp.bfloat16)
    fetched = latent[dest]
    hidden_dec = jax.nn.silu(jnp.dot(grid, dec_grid, preferred_element_type=jnp.float32) + jnp.dot(fetched, dec_mesh, preferred_element_type=jnp.float32)).astype(jnp.bfloat16)
    return jnp.dot(hidden_dec, dec_out, preferred_element_type=jnp.float32).astype(jnp.bfloat16)
```

```python
import functools

import jax
import jax.numpy as jnp
from jax import lax
from jax.experimental import pallas as pl
from jax.experimental.pallas import tpu as pltpu
from jax.sharding import PartitionSpec as P

L = 2
AXES = ("dom", "feat")
F32, BF16 = jnp.float32, jnp.bfloat16
MIB = 1 << 20


def silu(x):
    half = 0.5 * x
    return half + half * jnp.tanh(half)


def dot(a, b):
    return jnp.dot(a, b, preferred_element_type=F32)


def slot_codes(owner, node, parts, mesh_rows):
    core = lax.axis_index("feat")
    me = lax.axis_index("dom") * 2 + core
    slot = (owner - me) * (1 - 2 * core) + 2
    slot = jnp.where(slot < 0, slot + parts, slot)
    slot = jnp.where(slot >= parts, slot - parts, slot)
    return slot * mesh_rows + node


def one_hot_down(code, first, rows):
    n = code.shape[1]
    at = lax.broadcasted_iota(jnp.int32, (rows, n), 0)
    return jnp.where(at == code - first, 1.0, 0.0).astype(BF16)


def columns(row):
    n = row.shape[1]
    row = row.astype(F32)
    parts = [
        jnp.broadcast_to(row[:, i : i + 128], (128, 128)).T for i in range(0, n, 128)
    ]
    return jnp.concatenate(parts, axis=0)


def one_hot_across(cols, first, width):
    at = lax.broadcasted_iota(jnp.int32, cols.shape, 1).astype(F32)
    blocks = [
        jnp.where(cols == at + float(first + i), 1.0, 0.0).astype(BF16)
        for i in range(0, width, 128)
    ]
    return jnp.concatenate(blocks, axis=1)


def encode_kernel(parts, mesh_rows, owner, node, grid, w1, bias, hidden, near, cross, acc):
    step = pl.program_id(0)
    code = slot_codes(owner[...], node[...], parts, mesh_rows)
    h = silu(dot(grid[...], w1[...]) + bias[...]).astype(BF16)
    hidden[...] = h
    sums = dot(one_hot_down(code, 0, 2 * mesh_rows), h)

    @pl.when(step == 0)
    def _():
        acc[...] = sums

    @pl.when(step > 0)
    def _():
        acc[...] += sums

    @pl.when(step == pl.num_programs(0) - 1)
    def _():
        near[...] = acc[:mesh_rows].astype(BF16)
        cross[...] = acc[mesh_rows:].astype(BF16)


def far_kernel(parts, mesh_rows, owner, node, hidden, crossed, far, acc):
    step = pl.program_id(0)
    code = slot_codes(owner[...], node[...], parts, mesh_rows)
    sums = dot(one_hot_down(code, 4 * mesh_rows, mesh_rows), hidden[...])

    @pl.when(step == 0)
    def _():
        acc[...] = sums + crossed[...].astype(F32)

    @pl.when(step > 0)
    def _():
        acc[...] += sums

    @pl.when(step == pl.num_programs(0) - 1)
    def _():
        far[...] = acc[...].astype(BF16)


def chip_kernel(parts, mesh_rows, owner, node, hidden, own, sibling, acc):
    step = pl.program_id(0)
    code = slot_codes(owner[...], node[...], parts, mesh_rows)
    sums = dot(one_hot_down(code, 2 * mesh_rows, 2 * mesh_rows), hidden[...])

    @pl.when(step == 0)
    def _():
        acc[...] = sums

    @pl.when(step > 0)
    def _():
        acc[...] += sums

    @pl.when(step == pl.num_programs(0) - 1)
    def _():
        own[...] = acc[:mesh_rows]
        sibling[...] = acc[mesh_rows:].astype(BF16)


def pick(index, table):
    one_hot = one_hot_down(index, 0, table.shape[0])
    out = lax.dot_general(one_hot, table, (((0,), (0,)), ((), ())), preferred_element_type=F32)
    return out.astype(BF16)


def latent_kernel(mesh, own, sibling, near, far, w2, halo_index, latent, halo):
    sums = own[...] + sibling[...].astype(F32) + near[...].astype(F32) + far[...].astype(F32)
    rows = (mesh[...].astype(F32) + dot(sums.astype(BF16), w2[...])).astype(BF16)
    latent[...] = rows
    halo[...] = pick(halo_index[...], rows)


def project_kernel(latent, w_src, w_dst, bias, source, target):
    source[...] = dot(latent[...], w_src[0]).astype(BF16)
    target[...] = dot(latent[...], w_dst[0]) + bias[0]


def layer_kernel(last, latent, source, target, across, beside, edges, w_src, w_out, w_next, *outs):
    core = lax.axis_index("feat")
    halo_across = dot(across[...], w_src[0]).astype(BF16)
    halo_beside = dot(beside[...], w_src[0]).astype(BF16)
    first = core == 0
    before = jnp.where(first, halo_across, halo_beside)
    after = jnp.where(first, halo_beside, halo_across)
    table = jnp.concatenate([source[...], before, after], axis=0)
    total = None
    for k in range(edges.shape[0]):
        one_hot = one_hot_across(columns(edges[k : k + 1, :]), 0, table.shape[0])
        message = silu(dot(one_hot, table) + target[...]).astype(BF16).astype(F32)
        total = message if total is None else total + message
    rows = latent[...].astype(F32) + dot(total.astype(BF16), w_out[0])
    rows = rows.astype(BF16)
    if last:
        outs[0][...] = dot(rows, w_next[...]).astype(BF16)
    else:
        outs[0][...] = rows
        outs[1][...] = pick(w_next[...], rows)


def base_kernel(parts, mesh_rows, owner, node, grid, w_grid, own, sibling, base):
    cols = columns(slot_codes(owner[...], node[...], parts, mesh_rows))
    out = dot(grid[...], w_grid[...])
    out += dot(one_hot_across(cols, 2 * mesh_rows, mesh_rows), own[...])
    out += dot(one_hot_across(cols, 3 * mesh_rows, mesh_rows), sibling[...])
    base[...] = out.astype(BF16)


def decode_kernel(parts, mesh_rows, owner, node, base, near, cross, far, w_out, out):
    cols = columns(slot_codes(owner[...], node[...], parts, mesh_rows))
    pre = base[...].astype(F32)
    pre += dot(one_hot_across(cols, 0, mesh_rows), near[...])
    pre += dot(one_hot_across(cols, mesh_rows, mesh_rows), cross[...])
    pre += dot(one_hot_across(cols, 4 * mesh_rows, mesh_rows), far[...])
    out[...] = dot(silu(pre).astype(BF16), w_out[...]).astype(BF16)


def whole(shape):
    return pl.BlockSpec(shape, lambda *_: (0,) * len(shape))


def call(kernel, grid, ins, outs, flops, scratch=(), vmem=24):
    moved = sum(a.size * a.dtype.itemsize for a, _ in ins)
    return pl.pallas_call(
        kernel,
        grid=grid,
        in_specs=[spec for _, spec in ins],
        out_specs=[spec for _, _, spec in outs],
        out_shape=[jax.ShapeDtypeStruct(shape, dtype) for shape, dtype, _ in outs],
        scratch_shapes=list(scratch),
        compiler_params=pltpu.CompilerParams(vmem_limit_bytes=vmem * MIB),
        cost_estimate=pl.CostEstimate(flops=flops, bytes_accessed=moved, transcendentals=0),
    )(*[a for a, _ in ins])


def body(
    grid,
    mesh_feat,
    owner,
    node,
    halo_index,
    edge_src,
    w_enc1,
    enc_bias,
    w_enc2,
    proc_src,
    proc_dst,
    proc_bias,
    proc_out,
    dec_grid,
    dec_mesh,
    dec_out,
):
    parts = lax.axis_size(AXES)
    rows, width = grid.shape
    mesh_rows = mesh_feat.shape[0]
    border = halo_index.shape[0]
    degree = edge_src.shape[1]
    block = 512
    steps = (rows // block,)

    def sided(step):
        return [(i, (i + step) % parts if i % 2 == 0 else (i - step) % parts) for i in range(parts)]

    def swap(value):
        return lax.ppermute(value, AXES, sided(1))

    def across(value):
        return lax.ppermute(value, AXES, sided(-1))

    def to_near(value):
        return lax.ppermute(value, AXES, sided(-2))

    def to_far(value):
        return lax.ppermute(value, AXES, sided(2))

    owner = owner.reshape(1, rows)
    node = node.reshape(1, rows)
    halo_index = halo_index.reshape(1, border)
    edges = edge_src.T
    enc_bias = enc_bias.reshape(1, width)
    proc_bias = proc_bias.reshape(L, 1, width)

    by_lane = pl.BlockSpec((1, block), lambda i: (0, i))
    by_row = pl.BlockSpec((block, width), lambda i: (i, 0))
    square = whole((width, width))
    table = whole((mesh_rows, width))
    part = functools.partial

    unit = 2 * rows * width
    hidden, near, cross = call(
        part(encode_kernel, parts, mesh_rows),
        steps,
        [(owner, by_lane), (node, by_lane), (grid, by_row), (w_enc1, square), (enc_bias, whole((1, width)))],
        [((rows, width), BF16, by_row), ((mesh_rows, width), BF16, table), ((mesh_rows, width), BF16, table)],
        unit * (width + 2 * mesh_rows),
        [pltpu.VMEM((2 * mesh_rows, width), F32)],
    )
    crossed = swap(cross)
    near = to_near(near)
    (far,) = call(
        part(far_kernel, parts, mesh_rows),
        steps,
        [(owner, by_lane), (node, by_lane), (hidden, by_row), (crossed, table)],
        [((mesh_rows, width), BF16, table)],
        unit * mesh_rows,
        [pltpu.VMEM((mesh_rows, width), F32)],
    )
    far = to_far(far)
    own, sibling = call(
        part(chip_kernel, parts, mesh_rows),
        steps,
        [(owner, by_lane), (node, by_lane), (hidden, by_row)],
        [((mesh_rows, width), F32, table), ((mesh_rows, width), BF16, table)],
        unit * 2 * mesh_rows,
        [pltpu.VMEM((2 * mesh_rows, width), F32)],
    )
    sibling = swap(sibling)
    halo_rows = whole((border, width))
    latent, halo = call(
        latent_kernel,
        (1,),
        [(mesh_feat, table), (own, table), (sibling, table), (near, table), (far, table), (w_enc2, square), (halo_index, whole((1, border)))],
        [((mesh_rows, width), BF16, table), ((border, width), BF16, halo_rows)],
        2 * mesh_rows * width * width,
    )
    for layer in range(L):
        last = layer == L - 1
        halo_across = across(halo)
        halo_beside = swap(halo)
        weights = pl.BlockSpec((1, width, width), lambda i, layer=layer: (layer, 0, 0))
        source, target = call(
            project_kernel,
            (1,),
            [(latent, table), (proc_src, weights), (proc_dst, weights), (proc_bias, pl.BlockSpec((1, 1, width), lambda i, layer=layer: (layer, 0, 0)))],
            [((mesh_rows, width), BF16, table), ((mesh_rows, width), F32, table)],
            4 * mesh_rows * width * width,
        )
        following = (dec_mesh, square) if last else (halo_index, whole((1, border)))
        outs = [((mesh_rows, width), BF16, table)]
        if not last:
            outs.append(((border, width), BF16, halo_rows))
        made = call(
            part(layer_kernel, last),
            (1,),
            [
                (latent, table),
                (source, table),
                (target, table),
                (halo_across, halo_rows),
                (halo_beside, halo_rows),
                (edges, whole((degree, mesh_rows))),
                (proc_src, weights),
                (proc_out, weights),
                following,
            ],
            outs,
            2 * mesh_rows * width * (degree * 2 * mesh_rows + 2 * width),
        )
        if last:
            (projected,) = made
        else:
            latent, halo = made
    sibling = swap(projected)
    far = to_near(projected)
    near = to_far(projected)
    cross = swap(far)
    (base,) = call(
        part(base_kernel, parts, mesh_rows),
        steps,
        [(owner, by_lane), (node, by_lane), (grid, by_row), (dec_grid, square), (projected, table), (sibling, table)],
        [((rows, width), BF16, by_row)],
        unit * (width + 2 * mesh_rows),
    )
    (out,) = call(
        part(decode_kernel, parts, mesh_rows),
        steps,
        [(owner, by_lane), (node, by_lane), (base, by_row), (near, table), (cross, table), (far, table), (dec_out, square)],
        [((rows, width), BF16, by_row)],
        unit * (width + 3 * mesh_rows),
    )
    return out


def solution(mesh):
    rows = P(("group", "dom", "feat"), None)
    flat = P(("group", "dom", "feat"))
    return jax.shard_map(
        body,
        mesh=mesh,
        in_specs=(rows, rows, rows, flat, flat, rows) + (P(),) * 10,
        out_specs=rows,
        check_vma=False,
    )
```

```python
import functools

import jax
import jax.numpy as jnp
from jax import lax
from jax.experimental import pallas as pl
from jax.experimental.pallas import tpu as pltpu
from jax.sharding import PartitionSpec as P

L = 2
AXES = ("dom", "feat")
F32, BF16 = jnp.float32, jnp.bfloat16
MIB = 1 << 20
BLOCK = 512


def silu(x):
    half = 0.5 * x
    return half + half * jnp.tanh(half)


def dot(a, b):
    return jnp.dot(a, b, preferred_element_type=F32)


def slot_codes(owner, node, parts, mesh_rows):
    core = lax.axis_index("feat")
    me = lax.axis_index("dom") * 2 + core
    slot = (owner - me) * (1 - 2 * core) + 2
    slot = jnp.where(slot < 0, slot + parts, slot)
    slot = jnp.where(slot >= parts, slot - parts, slot)
    return slot * mesh_rows + node


def one_hot_down(code, first, rows):
    at = lax.broadcasted_iota(jnp.int32, (rows, code.shape[1]), 0)
    return jnp.where(at == code - first, 1.0, 0.0).astype(BF16)


def one_hot_across(row, width):
    n = row.shape[1]
    row = row.astype(F32)
    made = []
    for i in range(0, n, 128):
        cols = jnp.broadcast_to(row[:, i : i + 128], (128, 128)).T
        at = lax.broadcasted_iota(jnp.int32, cols.shape, 1).astype(F32)
        made.append(
            jnp.concatenate(
                [jnp.where(cols == at + float(j), 1.0, 0.0).astype(BF16) for j in range(0, width, 128)],
                axis=1,
            )
        )
    return jnp.concatenate(made, axis=0)


def encode_kernel(parts, owner, node, grid, w1, bias, hidden, near, cross, code, owner_v, node_v, grid_v, w1_v, bias_v, sems):
    small = [(owner, owner_v), (node, node_v), (w1, w1_v), (bias, bias_v)]
    copies = [pltpu.make_async_copy(a, b, sems.at[i]) for i, (a, b) in enumerate(small)]
    starts = range(0, grid.shape[0], BLOCK)
    blocks = [
        pltpu.make_async_copy(grid.at[pl.ds(r, BLOCK)], grid_v.at[pl.ds(r, BLOCK)], sems.at[4 + i])
        for i, r in enumerate(starts)
    ]
    for copy in copies + blocks:
        copy.start()
    for copy in copies:
        copy.wait()
    mesh_rows = near.shape[0]
    code[...] = slot_codes(owner_v[...], node_v[...], parts, mesh_rows)
    for r, copy in zip(starts, blocks):
        copy.wait()
        hidden[r : r + BLOCK] = silu(dot(grid_v[r : r + BLOCK], w1_v[...]) + bias_v[...]).astype(BF16)
    cross[...] = dot(one_hot_down(code[...], mesh_rows, mesh_rows), hidden[...]).astype(BF16)
    near[...] = dot(one_hot_down(code[...], 0, mesh_rows), hidden[...]).astype(BF16)


def far_kernel(code, hidden, crossed, far):
    rows = far.shape[0]
    far[...] = (dot(one_hot_down(code[...], 4 * rows, rows), hidden[...]) + crossed[...].astype(F32)).astype(BF16)


def chip_kernel(after, code, hidden, own, sibling):
    del after
    rows = own.shape[0]
    sibling[...] = dot(one_hot_down(code[...], 3 * rows, rows), hidden[...]).astype(BF16)
    own[...] = dot(one_hot_down(code[...], 2 * rows, rows), hidden[...])


def prepare_kernel(after, code, edges, halo_index, fetch, gather, gather_halo, pick):
    del after
    width = fetch.shape[1]
    for r in range(0, fetch.shape[0], BLOCK):
        fetch[r : r + BLOCK] = one_hot_across(code[:, r : r + BLOCK], width)
    n = edges.shape[1]
    own = gather.shape[1]
    for k in range(edges.shape[0]):
        one_hot = one_hot_across(edges[k : k + 1, :], own + gather_halo.shape[1])
        gather[k * n : (k + 1) * n] = one_hot[:, :own]
        gather_halo[k * n : (k + 1) * n] = one_hot[:, own:]
    pick[...] = one_hot_down(halo_index[...], 0, n)


def picked(pick, rows):
    return lax.dot_general(pick, rows, (((0,), (0,)), ((), ())), preferred_element_type=F32).astype(BF16)


def latent_kernel(mesh, own, sibling, near, far, w2, pick, latent, halo):
    sums = own[...] + sibling[...].astype(F32) + near[...].astype(F32) + far[...].astype(F32)
    rows = (mesh[...].astype(F32) + dot(sums.astype(BF16), w2[...])).astype(BF16)
    latent[...] = rows
    halo[...] = picked(pick[...], rows)


def project_kernel(layer, latent, w_src, w_dst, bias, gather, before):
    n = latent.shape[0]
    source = dot(latent[...], w_src[layer]).astype(BF16)
    target = dot(latent[...], w_dst[layer]) + bias[layer : layer + 1]
    for k in range(gather.shape[0] // n):
        before[k * n : (k + 1) * n] = dot(gather[k * n : (k + 1) * n], source) + target


def layer_kernel(layer, latent, before, across, beside, gather_halo, w_src, w_out, following, *outs):
    first = lax.axis_index("feat") == 0
    down = jnp.where(first, across[...], beside[...])
    up = jnp.where(first, beside[...], across[...])
    table = dot(jnp.concatenate([down, up], axis=0), w_src[layer]).astype(BF16)
    n = latent.shape[0]
    total = None
    for k in range(before.shape[0] // n):
        spot = slice(k * n, (k + 1) * n)
        message = silu(dot(gather_halo[spot], table) + before[spot]).astype(BF16).astype(F32)
        total = message if total is None else total + message
    rows = (latent[...].astype(F32) + dot(total.astype(BF16), w_out[layer])).astype(BF16)
    if layer == L - 1:
        outs[0][...] = dot(rows, following[...]).astype(BF16)
    else:
        outs[0][...] = rows
        outs[1][...] = picked(following[...], rows)


def base_kernel(grid, w_grid, fetch, own, sibling, base, stacked):
    width, rows = w_grid.shape[0], own.shape[0]
    stacked[:rows] = own[...]
    stacked[rows:] = sibling[...]
    for r in range(0, grid.shape[0], BLOCK):
        spot = slice(r, r + BLOCK)
        base[spot] = dot(grid[spot], w_grid[...]) + dot(fetch[spot, 2 * rows : 4 * rows], stacked[...])


def add_kernel(slot, fetch, base, table, out, *passed):
    rows = table.shape[0]
    for r in range(0, base.shape[0], BLOCK):
        spot = slice(r, r + BLOCK)
        out[spot] = base[spot] + dot(fetch[spot, slot * rows : (slot + 1) * rows], table[...])
    if passed:
        passed[0][...] = table[...]


def decode_kernel(slot, fetch, base, table, w_out, out, out_v, sems):
    rows = table.shape[0]
    copies = []
    for i, r in enumerate(range(0, base.shape[0], BLOCK)):
        spot = slice(r, r + BLOCK)
        hidden = silu(base[spot] + dot(fetch[spot, slot * rows : (slot + 1) * rows], table[...])).astype(BF16)
        out_v[spot] = dot(hidden, w_out[...]).astype(BF16)
        copies.append(pltpu.make_async_copy(out_v.at[pl.ds(r, BLOCK)], out.at[pl.ds(r, BLOCK)], sems.at[i]))
        copies[-1].start()
    for copy in copies:
        copy.wait()


VM = pltpu.VMEM


def call(kernel, ins, outs, flops, scratch=(), vmem=24, spaces=None, out_space=VM):
    moved = sum(a.size * a.dtype.itemsize for a in ins)
    spaces = spaces or [VM] * len(ins)
    ins = [pltpu.with_memory_space_constraint(a, s) if s is pltpu.HBM else a for a, s in zip(ins, spaces)]
    return pl.pallas_call(
        kernel,
        in_specs=[pl.BlockSpec(memory_space=space) for space in spaces],
        out_specs=[pl.BlockSpec(memory_space=out_space) for _ in outs],
        out_shape=[jax.ShapeDtypeStruct(shape, dtype) for shape, dtype in outs],
        scratch_shapes=list(scratch),
        compiler_params=pltpu.CompilerParams(vmem_limit_bytes=vmem * MIB),
        cost_estimate=pl.CostEstimate(flops=flops, bytes_accessed=moved if flops > 1 else 1, transcendentals=0),
    )(*ins)


def body(
    grid,
    mesh_feat,
    owner,
    node,
    halo_index,
    edge_src,
    w_enc1,
    enc_bias,
    w_enc2,
    proc_src,
    proc_dst,
    proc_bias,
    proc_out,
    dec_grid,
    dec_mesh,
    dec_out,
):
    parts = lax.axis_size(AXES)
    rows, width = grid.shape
    mesh_rows = mesh_feat.shape[0]
    border = halo_index.shape[0]
    degree = edge_src.shape[1]
    blocks = rows // BLOCK
    part = functools.partial

    def sided(step):
        return [(i, (i + step) % parts if i % 2 == 0 else (i - step) % parts) for i in range(parts)]

    def swap(value):
        return lax.ppermute(value, AXES, sided(1))

    def to_across(value):
        return lax.ppermute(value, AXES, sided(-1))

    def to_near(value):
        return lax.ppermute(value, AXES, sided(-2))

    def to_far(value):
        return lax.ppermute(value, AXES, sided(2))

    table = ((mesh_rows, width), BF16)
    unit = 2 * rows * width
    hidden, near, cross, code = call(
        part(encode_kernel, parts),
        [owner.reshape(1, rows), node.reshape(1, rows), grid, w_enc1, enc_bias.reshape(1, width)],
        [((rows, width), BF16), table, table, ((1, rows), jnp.int32)],
        unit * (width + 2 * mesh_rows),
        [
            VM((1, rows), jnp.int32),
            VM((1, rows), jnp.int32),
            VM((rows, width), BF16),
            VM((width, width), BF16),
            VM((1, width), F32),
            pltpu.SemaphoreType.DMA((4 + blocks,)),
        ],
        spaces=[pltpu.HBM] * 5,
    )
    crossed = swap(cross)
    near = to_near(near)
    (sent,) = call(far_kernel, [code, hidden, crossed], [table], unit * mesh_rows)
    far = to_far(sent)
    own, sibling = call(
        chip_kernel,
        [sent, code, hidden],
        [((mesh_rows, width), F32), table],
        unit * 2 * mesh_rows,
        spaces=[pl.ANY, VM, VM],
    )
    fetch, gather, gather_halo, pick = call(
        prepare_kernel,
        [sibling, code, edge_src.T, halo_index.reshape(1, border)],
        [
            ((rows, 5 * mesh_rows), BF16),
            ((degree * mesh_rows, mesh_rows), BF16),
            ((degree * mesh_rows, 2 * border), BF16),
            ((mesh_rows, border), BF16),
        ],
        unit * 2 * mesh_rows,
        spaces=[pl.ANY, VM, VM, VM],
    )
    sibling = swap(sibling)
    latent, halo = call(
        latent_kernel,
        [mesh_feat, own, sibling, near, far, w_enc2, pick],
        [table, ((border, width), BF16)],
        2 * mesh_rows * width * width,
    )
    for layer in range(L):
        last = layer == L - 1
        across = to_across(halo)
        beside = swap(halo)
        (before,) = call(
            part(project_kernel, layer),
            [latent, proc_src, proc_dst, proc_bias, gather],
            [((degree * mesh_rows, width), F32)],
            4 * mesh_rows * width * width + 2 * degree * mesh_rows * mesh_rows * width,
        )
        made = call(
            part(layer_kernel, layer),
            [latent, before, across, beside, gather_halo, proc_src, proc_out, dec_mesh if last else pick],
            [table] if last else [table, ((border, width), BF16)],
            2 * mesh_rows * width * (degree * 2 * border + 2 * width),
        )
        if last:
            (projected,) = made
        else:
            latent, halo = made
    far = to_near(projected)
    sibling = swap(projected)
    near = to_far(projected)
    f32_rows = ((rows, width), F32)
    (base,) = call(
        base_kernel,
        [grid, dec_grid, fetch, projected, sibling],
        [f32_rows],
        1,
        [VM((2 * mesh_rows, width), BF16)],
    )
    base, passed = call(part(add_kernel, 4), [fetch, base, far], [f32_rows, table], 1)
    cross = swap(passed)
    (base,) = call(part(add_kernel, 0), [fetch, base, near], [f32_rows], 1)
    (out,) = call(
        part(decode_kernel, 1),
        [fetch, base, cross, dec_out],
        [((rows, width), BF16)],
        unit * (width + mesh_rows),
        [VM((rows, width), BF16), pltpu.SemaphoreType.DMA((blocks,))],
        out_space=pltpu.HBM,
    )
    return out


def solution(mesh):
    rows = P(("group", "dom", "feat"), None)
    flat = P(("group", "dom", "feat"))
    return jax.shard_map(
        body,
        mesh=mesh,
        in_specs=(rows, rows, rows, flat, flat, rows) + (P(),) * 10,
        out_specs=rows,
        check_vma=False,
    )
```

```python
import functools

import jax
import jax.numpy as jnp
from jax import lax
from jax.experimental import pallas as pl
from jax.experimental.pallas import tpu as pltpu
from jax.sharding import PartitionSpec as P

L = 2
AXES = ("dom", "feat")
F32, BF16 = jnp.float32, jnp.bfloat16
MIB = 1 << 20
BLOCK = 512
ENCODE_BLOCK = 512
DECODE_BLOCK = 256
LONG = 40_000_000_000


def silu_of_twice(half):
    return half + half * jnp.tanh(half)


def dot(a, b):
    return jnp.dot(a, b, preferred_element_type=F32)


def slot_codes(owner, node, parts, mesh_rows):
    core = lax.axis_index("feat")
    me = lax.axis_index("dom") * 2 + core
    slot = (owner - me) * (1 - 2 * core) + 2
    slot = jnp.where(slot < 0, slot + parts, slot)
    slot = jnp.where(slot >= parts, slot - parts, slot)
    return slot * mesh_rows + node


def one_hot_down(code, first, rows):
    at = lax.broadcasted_iota(jnp.int32, (rows, code.shape[1]), 0)
    return jnp.where(at == code - first, 1.0, 0.0).astype(BF16)


def one_hot_across(row, width):
    n = row.shape[1]
    row = row.astype(F32)
    made = []
    for i in range(0, n, 128):
        cols = jnp.broadcast_to(row[:, i : i + 128], (128, 128)).T
        at = lax.broadcasted_iota(jnp.int32, cols.shape, 1).astype(F32)
        made.append(
            jnp.concatenate(
                [jnp.where(cols == at + float(j), 1.0, 0.0).astype(BF16) for j in range(0, width, 128)],
                axis=1,
            )
        )
    return jnp.concatenate(made, axis=0)


def encode_kernel(parts, owner, node, grid, w1, bias, hidden, near, code, owner_v, node_v, grid_v, w1_v, bias_v, one_hot, sems):
    small = [(owner, owner_v), (node, node_v), (w1, w1_v), (bias, bias_v)]
    copies = [pltpu.make_async_copy(a, b, sems.at[i]) for i, (a, b) in enumerate(small)]
    starts = range(0, grid.shape[0], ENCODE_BLOCK)
    blocks = [
        pltpu.make_async_copy(grid.at[pl.ds(r, ENCODE_BLOCK)], grid_v.at[pl.ds(r, ENCODE_BLOCK)], sems.at[4 + i])
        for i, r in enumerate(starts)
    ]
    for copy in copies + blocks:
        copy.start()
    copies[0].wait()
    copies[1].wait()
    code[...] = slot_codes(owner_v[...], node_v[...], parts, near.shape[0])
    one_hot[...] = one_hot_down(code[...], 0, near.shape[0])
    copies[2].wait()
    copies[3].wait()
    weights = w1_v[...] * 0.5
    offset = bias_v[...] * 0.5
    for r, copy in zip(starts, blocks):
        copy.wait()
        spot = slice(r, r + ENCODE_BLOCK)
        hidden[spot] = silu_of_twice(dot(grid_v[spot], weights) + offset).astype(BF16)
    near[...] = dot(one_hot[...], hidden[...]).astype(BF16)


def cross_kernel(code, hidden, cross):
    rows = cross.shape[0]
    cross[...] = dot(one_hot_down(code[...], rows, rows), hidden[...]).astype(BF16)


def far_kernel(code, hidden, crossed, far):
    rows = far.shape[0]
    far[...] = (dot(one_hot_down(code[...], 4 * rows, rows), hidden[...]) + crossed[...].astype(F32)).astype(BF16)


def chip_kernel(after, code, hidden, own, sibling):
    del after
    rows = own.shape[0]
    sibling[...] = dot(one_hot_down(code[...], 3 * rows, rows), hidden[...]).astype(BF16)
    own[...] = dot(one_hot_down(code[...], 2 * rows, rows), hidden[...])


def prepare_kernel(after, code, edges, halo_index, fetch, gather, gather_halo, pick, lead, lead_halo):
    del after
    width = fetch.shape[1]
    for r in range(0, fetch.shape[0], BLOCK):
        fetch[r : r + BLOCK] = one_hot_across(code[:, r : r + BLOCK], width)
    n, own = edges.shape[1], gather.shape[1]
    border = halo_index.shape[1]
    pick[...] = one_hot_down(halo_index[...], 0, n)
    for k in range(edges.shape[0]):
        one_hot = one_hot_across(edges[k : k + 1, :], own + gather_halo.shape[1])
        gather[k * n : (k + 1) * n] = one_hot[:, :own]
        gather_halo[k * n : (k + 1) * n] = one_hot[:, own:]
        ahead = picked(pick[...], one_hot)
        lead[k * border : (k + 1) * border] = ahead[:, :own]
        lead_halo[k * border : (k + 1) * border] = ahead[:, own:]


def picked(pick, rows):
    return lax.dot_general(pick, rows, (((0,), (0,)), ((), ())), preferred_element_type=F32).astype(BF16)


def latent_kernel(mesh, own, sibling, near, far, w2, pick, latent, halo):
    sums = own[...] + sibling[...].astype(F32) + near[...].astype(F32) + far[...].astype(F32)
    rows = (mesh[...].astype(F32) + dot(sums.astype(BF16), w2[...])).astype(BF16)
    latent[...] = rows
    halo[...] = picked(pick[...], rows)


def own_terms(layer, nodes, gather, source, w_dst, bias, before):
    n = nodes.shape[0]
    target = dot(nodes[...], w_dst[layer]) * 0.5 + bias[layer : layer + 1] * 0.5
    for k in range(gather.shape[0] // n):
        before[k * n : (k + 1) * n] = dot(gather[k * n : (k + 1) * n], source) + target


def project_kernel(layer, latent, w_src, w_dst, bias, gather, halo, *more):
    source = (dot(latent[...], w_src[layer]) * 0.5).astype(BF16)
    if len(more) > 2:
        lead, before, passed, before_lead = more
        own_terms(layer, halo, lead, source, w_dst, bias, before_lead)
    else:
        before, passed = more
    passed[...] = halo[...]
    own_terms(layer, latent, gather, source, w_dst, bias, before)


def halo_table(layer, across, beside, w_src):
    first = lax.axis_index("feat") == 0
    down = jnp.where(first, across[...], beside[...])
    up = jnp.where(first, beside[...], across[...])
    return (dot(jnp.concatenate([down, up], axis=0), w_src[layer]) * 0.5).astype(BF16)


def updated(layer, nodes, before, gather_halo, table, w_out):
    n = nodes.shape[0]
    total = None
    for k in range(before.shape[0] // n):
        spot = slice(k * n, (k + 1) * n)
        message = silu_of_twice(dot(gather_halo[spot], table) + before[spot])
        total = message if total is None else total + message
    return (nodes[...].astype(F32) + dot(total.astype(BF16), w_out[layer])).astype(BF16)


def lead_kernel(layer, halo, before, across, beside, gather_halo, w_src, w_out, new_halo, table):
    table[...] = halo_table(layer, across, beside, w_src)
    new_halo[...] = updated(layer, halo, before, gather_halo, table[...], w_out)


def layer_kernel(layer, latent, before, table, gather_halo, w_out, new):
    new[...] = updated(layer, latent, before, gather_halo, table[...], w_out)


def last_layer_kernel(layer, latent, before, across, beside, gather_halo, w_src, w_out, w_mesh, projected):
    table = halo_table(layer, across, beside, w_src)
    rows = updated(layer, latent, before, gather_halo, table, w_out)
    projected[...] = (dot(rows, w_mesh[...]) * 0.5).astype(BF16)


def base_kernel(grid, w_grid, fetch, own, base, passed):
    rows = own.shape[0]
    passed[...] = own[...]
    for r in range(0, grid.shape[0], BLOCK):
        spot = slice(r, r + BLOCK)
        base[spot] = dot(grid[spot], w_grid[...]) * 0.5 + dot(fetch[spot, 2 * rows : 3 * rows], own[...])


def add_kernel(fetch, base, sibling, far, out, stacked):
    rows = far.shape[0]
    stacked[:rows] = sibling[...]
    stacked[rows:] = far[...]
    for r in range(0, base.shape[0], BLOCK):
        spot = slice(r, r + BLOCK)
        out[spot] = base[spot] + dot(fetch[spot, 3 * rows : 5 * rows], stacked[...])


def pass_kernel(table, out):
    out[...] = table[...]


def decode_kernel(fetch, base, *refs):
    *tables, w_out, out, stacked, out_v, sems = refs
    rows = tables[0].shape[0]
    for i, table in enumerate(tables):
        stacked[i * rows : (i + 1) * rows] = table[...]
    def halved(r):
        spot = slice(r, r + DECODE_BLOCK)
        return base[spot] + dot(fetch[spot, : stacked.shape[0]], stacked[...])

    copies = []
    half = halved(0)
    for i, r in enumerate(range(0, base.shape[0], DECODE_BLOCK)):
        ahead = halved(r + DECODE_BLOCK) if r + DECODE_BLOCK < base.shape[0] else None
        out_v[r : r + DECODE_BLOCK] = dot(silu_of_twice(half).astype(BF16), w_out[...]).astype(BF16)
        half = ahead
        copies.append(pltpu.make_async_copy(out_v.at[pl.ds(r, DECODE_BLOCK)], out.at[pl.ds(r, DECODE_BLOCK)], sems.at[i]))
        copies[-1].start()
    for copy in copies:
        copy.wait()


VM = pltpu.VMEM


def call(kernel, ins, outs, flops, scratch=(), vmem=24, spaces=None, out_space=VM):
    moved = sum(a.size * a.dtype.itemsize for a in ins)
    spaces = spaces or [VM] * len(ins)
    ins = [pltpu.with_memory_space_constraint(a, s) if s is pltpu.HBM else a for a, s in zip(ins, spaces)]
    return pl.pallas_call(
        kernel,
        in_specs=[pl.BlockSpec(memory_space=space) for space in spaces],
        out_specs=[pl.BlockSpec(memory_space=out_space) for _ in outs],
        out_shape=[jax.ShapeDtypeStruct(shape, dtype) for shape, dtype in outs],
        scratch_shapes=list(scratch),
        compiler_params=pltpu.CompilerParams(vmem_limit_bytes=vmem * MIB),
        cost_estimate=pl.CostEstimate(flops=flops, bytes_accessed=moved if flops > 1 else 1, transcendentals=0),
    )(*ins)


def body(
    grid,
    mesh_feat,
    owner,
    node,
    halo_index,
    edge_src,
    w_enc1,
    enc_bias,
    w_enc2,
    proc_src,
    proc_dst,
    proc_bias,
    proc_out,
    dec_grid,
    dec_mesh,
    dec_out,
):
    parts = lax.axis_size(AXES)
    rows, width = grid.shape
    mesh_rows = mesh_feat.shape[0]
    border = halo_index.shape[0]
    degree = edge_src.shape[1]
    part = functools.partial

    def sided(step):
        return [(i, (i + step) % parts if i % 2 == 0 else (i - step) % parts) for i in range(parts)]

    def swap(value):
        return lax.ppermute(value, AXES, sided(1))

    def to_across(value):
        return lax.ppermute(value, AXES, sided(-1))

    def to_near(value):
        return lax.ppermute(value, AXES, sided(-2))

    def to_far(value):
        return lax.ppermute(value, AXES, sided(2))

    table = ((mesh_rows, width), BF16)
    border_rows = ((border, width), BF16)
    unit = 2 * rows * width
    hidden, near, code = call(
        part(encode_kernel, parts),
        [owner.reshape(1, rows), node.reshape(1, rows), grid, w_enc1, enc_bias.reshape(1, width)],
        [((rows, width), BF16), table, ((1, rows), jnp.int32)],
        unit * (width + mesh_rows),
        [
            VM((1, rows), jnp.int32),
            VM((1, rows), jnp.int32),
            VM((rows, width), BF16),
            VM((width, width), BF16),
            VM((1, width), F32),
            VM((mesh_rows, rows), BF16),
            pltpu.SemaphoreType.DMA((4 + rows // ENCODE_BLOCK,)),
        ],
        spaces=[pltpu.HBM] * 5,
    )
    near = to_near(near)
    (cross,) = call(cross_kernel, [code, hidden], [table], 1)
    crossed = swap(cross)
    (sent,) = call(far_kernel, [code, hidden, crossed], [table], 1)
    far = to_far(sent)
    own, sibling = call(
        chip_kernel,
        [sent, code, hidden],
        [((mesh_rows, width), F32), table],
        unit * 2 * mesh_rows,
        spaces=[pl.ANY, VM, VM],
    )
    fetch, gather, gather_halo, pick, lead, lead_halo = call(
        prepare_kernel,
        [near, code, edge_src.T, halo_index.reshape(1, border)],
        [
            ((rows, 5 * mesh_rows), BF16),
            ((degree * mesh_rows, mesh_rows), BF16),
            ((degree * mesh_rows, 2 * border), BF16),
            ((mesh_rows, border), BF16),
            ((degree * border, mesh_rows), BF16),
            ((degree * border, 2 * border), BF16),
        ],
        LONG,
        spaces=[pl.ANY, VM, VM, VM],
    )
    sibling = swap(sibling)
    latent, halo = call(
        latent_kernel,
        [mesh_feat, own, sibling, near, far, w_enc2, pick],
        [table, border_rows],
        2 * mesh_rows * width * width,
    )
    edge_terms = ((degree * mesh_rows, width), F32)
    for layer in range(L - 1):
        across = to_across(halo)
        before, passed, before_lead = call(
            part(project_kernel, layer),
            [latent, proc_src, proc_dst, proc_bias, gather, halo, lead],
            [edge_terms, border_rows, ((degree * border, width), F32)],
            1,
        )
        beside = swap(passed)
        (across,) = call(pass_kernel, [across], [border_rows], LONG)
        halo, received = call(
            part(lead_kernel, layer),
            [halo, before_lead, across, beside, lead_halo, proc_src, proc_out],
            [border_rows, ((2 * border, width), BF16)],
            2 * border * width * (degree * 2 * border + 3 * width),
        )
        (latent,) = call(
            part(layer_kernel, layer),
            [latent, before, received, gather_halo, proc_out],
            [table],
            1,
        )
    across = to_across(halo)
    before, passed = call(
        part(project_kernel, L - 1),
        [latent, proc_src, proc_dst, proc_bias, gather, halo],
        [edge_terms, border_rows],
        1,
    )
    beside = swap(passed)
    (across,) = call(pass_kernel, [across], [border_rows], LONG)
    (projected,) = call(
        part(last_layer_kernel, L - 1),
        [latent, before, across, beside, gather_halo, proc_src, proc_out, dec_mesh],
        [table],
        2 * mesh_rows * width * (degree * 2 * border + 2 * width),
    )
    far = to_near(projected)
    f32_rows = ((rows, width), F32)
    base, passed = call(
        base_kernel,
        [grid, dec_grid, fetch, projected],
        [f32_rows, table],
        1,
    )
    near = to_far(passed)
    sibling = swap(passed)
    pair = [VM((2 * mesh_rows, width), BF16)]
    (far,) = call(pass_kernel, [far], [table], LONG)
    cross = swap(far)
    (base,) = call(add_kernel, [fetch, base, sibling, far], [f32_rows], 1, pair)
    (near,) = call(pass_kernel, [near], [table], LONG)
    tables = [near, cross]
    (out,) = call(
        decode_kernel,
        [fetch, base, *tables, dec_out],
        [((rows, width), BF16)],
        unit * (width + mesh_rows),
        [
            VM((len(tables) * mesh_rows, width), BF16),
            VM((rows, width), BF16),
            pltpu.SemaphoreType.DMA((rows // DECODE_BLOCK,)),
        ],
        out_space=pltpu.HBM,
    )
    return out


def solution(mesh):
    rows = P(("group", "dom", "feat"), None)
    flat = P(("group", "dom", "feat"))
    return jax.shard_map(
        body,
        mesh=mesh,
        in_specs=(rows, rows, rows, flat, flat, rows) + (P(),) * 10,
        out_specs=rows,
        check_vma=False,
    )
```

```python
import functools

import jax
import jax.numpy as jnp
from jax import lax
from jax.experimental import pallas as pl
from jax.experimental.pallas import tpu as pltpu
from jax.sharding import PartitionSpec as P

L = 2
AXES = ("dom", "feat")
F32, BF16 = jnp.float32, jnp.bfloat16
MIB = 1 << 20
BLOCK = 512
ENCODE_BLOCK = 1024
DECODE_BLOCK = 256
LONG = 40_000_000_000


def silu_of_twice(half):
    return half + half * jnp.tanh(half)


def dot(a, b):
    return jnp.dot(a, b, preferred_element_type=F32)


def slot_codes(owner, node, parts, mesh_rows):
    core = lax.axis_index("feat")
    me = lax.axis_index("dom") * 2 + core
    slot = (owner - me) * (1 - 2 * core) + 2
    slot = jnp.where(slot < 0, slot + parts, slot)
    slot = jnp.where(slot >= parts, slot - parts, slot)
    return slot * mesh_rows + node


def one_hot_down(code, first, rows):
    at = lax.broadcasted_iota(jnp.int32, (rows, code.shape[1]), 0)
    return jnp.where(at == code - first, 1.0, 0.0).astype(BF16)


def one_hot_across(row, width):
    n = row.shape[1]
    row = row.astype(F32)
    made = []
    for i in range(0, n, 128):
        cols = jnp.broadcast_to(row[:, i : i + 128], (128, 128)).T
        at = lax.broadcasted_iota(jnp.int32, cols.shape, 1).astype(F32)
        made.append(
            jnp.concatenate(
                [jnp.where(cols == at + float(j), 1.0, 0.0).astype(BF16) for j in range(0, width, 128)],
                axis=1,
            )
        )
    return jnp.concatenate(made, axis=0)


def encode_kernel(parts, owner, node, grid, w1, bias, hidden, near, cross, code, owner_v, node_v, grid_v, w1_v, bias_v, one_hot, sems):
    small = [(owner, owner_v), (node, node_v), (w1, w1_v), (bias, bias_v)]
    copies = [pltpu.make_async_copy(a, b, sems.at[i]) for i, (a, b) in enumerate(small)]
    starts = range(0, grid.shape[0], ENCODE_BLOCK)
    blocks = [
        pltpu.make_async_copy(grid.at[pl.ds(r, ENCODE_BLOCK)], grid_v.at[pl.ds(r, ENCODE_BLOCK)], sems.at[4 + i])
        for i, r in enumerate(starts)
    ]
    for copy in copies + blocks[:1]:
        copy.start()
    copies[0].wait()
    copies[1].wait()
    for copy in blocks[1:]:
        copy.start()
    code[...] = slot_codes(owner_v[...], node_v[...], parts, near.shape[0])
    one_hot[...] = one_hot_down(code[...], 0, one_hot.shape[0])
    copies[2].wait()
    copies[3].wait()
    weights = w1_v[...] * 0.5
    offset = bias_v[...] * 0.5
    for r, copy in zip(starts, blocks):
        copy.wait()
        spot = slice(r, r + ENCODE_BLOCK)
        hidden[spot] = silu_of_twice(dot(grid_v[spot], weights) + offset).astype(BF16)
    rows = near.shape[0]
    cross[...] = dot(one_hot[rows:], hidden[...]).astype(BF16)
    near[...] = dot(one_hot[:rows], hidden[...]).astype(BF16)


def far_kernel(code, hidden, crossed, far):
    rows = far.shape[0]
    far[...] = (dot(one_hot_down(code[...], 4 * rows, rows), hidden[...]) + crossed[...].astype(F32)).astype(BF16)


def chip_kernel(after, code, hidden, own, sibling):
    del after
    rows = own.shape[0]
    sibling[...] = dot(one_hot_down(code[...], 3 * rows, rows), hidden[...]).astype(BF16)
    own[...] = dot(one_hot_down(code[...], 2 * rows, rows), hidden[...])


def prepare_kernel(after, edges, halo_index, w_out, w_mesh, gather, gather_halo, pick, lead, lead_halo, joined):
    del after
    joined[...] = (dot(w_out[L - 1], w_mesh[...]) * 0.5).astype(BF16)
    n, own = edges.shape[1], gather.shape[1]
    border = halo_index.shape[1]
    pick[...] = one_hot_down(halo_index[...], 0, n)
    for k in range(edges.shape[0]):
        one_hot = one_hot_across(edges[k : k + 1, :], own + gather_halo.shape[1])
        gather[k * n : (k + 1) * n] = one_hot[:, :own]
        gather_halo[k * n : (k + 1) * n] = one_hot[:, own:]
        ahead = picked(pick[...], one_hot)
        lead[k * border : (k + 1) * border] = ahead[:, :own]
        lead_halo[k * border : (k + 1) * border] = ahead[:, own:]


def picked(pick, rows):
    return lax.dot_general(pick, rows, (((0,), (0,)), ((), ())), preferred_element_type=F32).astype(BF16)


def latent_kernel(mesh, own, sibling, near, far, w2, pick, latent, halo):
    sums = own[...] + sibling[...].astype(F32) + near[...].astype(F32) + far[...].astype(F32)
    rows = (mesh[...].astype(F32) + dot(sums.astype(BF16), w2[...])).astype(BF16)
    latent[...] = rows
    halo[...] = picked(pick[...], rows)


def own_terms(layer, nodes, gather, source, w_dst, bias, before):
    n = nodes.shape[0]
    target = dot(nodes[...], w_dst[layer]) * 0.5 + bias[layer : layer + 1] * 0.5
    for k in range(gather.shape[0] // n):
        before[k * n : (k + 1) * n] = dot(gather[k * n : (k + 1) * n], source) + target


def project_kernel(layer, latent, w_src, w_dst, bias, gather, halo, more_in, before, passed, more_out):
    source = (dot(latent[...], w_src[layer]) * 0.5).astype(BF16)
    if layer == L - 1:
        more_out[...] = dot(latent[...], more_in[...]) * 0.5
    else:
        own_terms(layer, halo, more_in, source, w_dst, bias, more_out)
    passed[...] = halo[...]
    own_terms(layer, latent, gather, source, w_dst, bias, before)


def halo_table(layer, across, beside, w_src):
    first = lax.axis_index("feat") == 0
    down = jnp.where(first, across[...], beside[...])
    up = jnp.where(first, beside[...], across[...])
    return (dot(jnp.concatenate([down, up], axis=0), w_src[layer]) * 0.5).astype(BF16)


def edge_sums(n, before, gather_halo, table):
    total = None
    for k in range(before.shape[0] // n):
        spot = slice(k * n, (k + 1) * n)
        message = silu_of_twice(dot(gather_halo[spot], table) + before[spot])
        total = message if total is None else total + message
    return total.astype(BF16)


def updated(layer, nodes, before, gather_halo, table, w_out):
    sums = edge_sums(nodes.shape[0], before, gather_halo, table)
    return (nodes[...].astype(F32) + dot(sums, w_out[layer])).astype(BF16)


def lead_kernel(layer, halo, before, across, beside, gather_halo, w_src, w_out, new_halo, table):
    table[...] = halo_table(layer, across, beside, w_src)
    new_halo[...] = updated(layer, halo, before, gather_halo, table[...], w_out)


def layer_kernel(layer, latent, before, table, gather_halo, w_out, new):
    new[...] = updated(layer, latent, before, gather_halo, table[...], w_out)


def last_layer_kernel(layer, before, across, beside, gather_halo, w_src, kept, joined, projected):
    sums = edge_sums(kept.shape[0], before, gather_halo, halo_table(layer, across, beside, w_src))
    projected[...] = (kept[...] + dot(sums, joined[...])).astype(BF16)


def base_kernel(code, grid, w_grid, own, fetch, base, *pieces):
    rows = own.shape[0]
    cut_kernel(own, *pieces)
    for r in range(0, grid.shape[0], BLOCK):
        spot = slice(r, r + BLOCK)
        fetch[spot] = one_hot_across(code[:, spot], fetch.shape[1])
        base[spot] = dot(grid[spot], w_grid[...]) * 0.5 + dot(fetch[spot, 2 * rows : 3 * rows], own[...])


def sibling_kernel(fetch, base, own, *refs):
    *pieces, out, passed = refs
    rows = own.shape[0]
    passed[...] = own[...]
    table = jnp.concatenate([piece[...] for piece in pieces], axis=0)
    for r in range(0, base.shape[0], BLOCK):
        spot = slice(r, r + BLOCK)
        out[spot] = base[spot] + dot(fetch[spot, 3 * rows : 4 * rows], table)


def far_add_kernel(fetch, base, far, out):
    rows = far.shape[0]
    for r in range(0, base.shape[0], BLOCK):
        spot = slice(r, r + BLOCK)
        out[spot] = base[spot] + dot(fetch[spot, 4 * rows : 5 * rows], far[...])


def cross_add_kernel(fetch, base, *refs):
    *pieces, out = refs
    table = jnp.concatenate([piece[...] for piece in pieces], axis=0)
    rows = table.shape[0]
    for r in range(0, base.shape[0], BLOCK):
        spot = slice(r, r + BLOCK)
        out[spot] = base[spot] + dot(fetch[spot, rows : 2 * rows], table)


def cut_kernel(table, *pieces):
    rows = pieces[0].shape[0]
    for i, piece in enumerate(pieces):
        piece[...] = table[i * rows : (i + 1) * rows]


def pass_kernel(table, out):
    out[...] = table[...]


def decode_kernel(fetch, base, *refs):
    *tables, w_out, out, stacked, out_v, sems = refs
    low = 0
    for table in tables:
        stacked[low : low + table.shape[0]] = table[...]
        low += table.shape[0]
    def halved(r):
        spot = slice(r, r + DECODE_BLOCK)
        return base[spot] + dot(fetch[spot, : stacked.shape[0]], stacked[...])

    copies = []
    half = halved(0)
    for i, r in enumerate(range(0, base.shape[0], DECODE_BLOCK)):
        ahead = halved(r + DECODE_BLOCK) if r + DECODE_BLOCK < base.shape[0] else None
        out_v[r : r + DECODE_BLOCK] = dot(silu_of_twice(half).astype(BF16), w_out[...]).astype(BF16)
        half = ahead
        copies.append(pltpu.make_async_copy(out_v.at[pl.ds(r, DECODE_BLOCK)], out.at[pl.ds(r, DECODE_BLOCK)], sems.at[i]))
        copies[-1].start()
    for copy in copies:
        copy.wait()


VM = pltpu.VMEM


def call(kernel, ins, outs, flops, scratch=(), vmem=24, spaces=None, out_space=VM):
    moved = sum(a.size * a.dtype.itemsize for a in ins)
    spaces = spaces or [VM] * len(ins)
    ins = [pltpu.with_memory_space_constraint(a, s) if s is pltpu.HBM else a for a, s in zip(ins, spaces)]
    return pl.pallas_call(
        kernel,
        in_specs=[pl.BlockSpec(memory_space=space) for space in spaces],
        out_specs=[pl.BlockSpec(memory_space=out_space) for _ in outs],
        out_shape=[jax.ShapeDtypeStruct(shape, dtype) for shape, dtype in outs],
        scratch_shapes=list(scratch),
        compiler_params=pltpu.CompilerParams(vmem_limit_bytes=vmem * MIB),
        cost_estimate=pl.CostEstimate(flops=flops, bytes_accessed=moved if flops > 1 else 1, transcendentals=0),
    )(*ins)


def body(
    grid,
    mesh_feat,
    owner,
    node,
    halo_index,
    edge_src,
    w_enc1,
    enc_bias,
    w_enc2,
    proc_src,
    proc_dst,
    proc_bias,
    proc_out,
    dec_grid,
    dec_mesh,
    dec_out,
):
    parts = lax.axis_size(AXES)
    rows, width = grid.shape
    mesh_rows = mesh_feat.shape[0]
    border = halo_index.shape[0]
    degree = edge_src.shape[1]
    part = functools.partial

    def sided(step):
        return [(i, (i + step) % parts if i % 2 == 0 else (i - step) % parts) for i in range(parts)]

    def swap(value):
        return lax.ppermute(value, AXES, sided(1))

    def to_across(value):
        return lax.ppermute(value, AXES, sided(-1))

    def to_near(value):
        return lax.ppermute(value, AXES, sided(-2))

    def to_far(value):
        return lax.ppermute(value, AXES, sided(2))

    table = ((mesh_rows, width), BF16)
    border_rows = ((border, width), BF16)
    unit = 2 * rows * width
    hidden, near, cross, code = call(
        part(encode_kernel, parts),
        [owner.reshape(1, rows), node.reshape(1, rows), grid, w_enc1, enc_bias.reshape(1, width)],
        [((rows, width), BF16), table, table, ((1, rows), jnp.int32)],
        unit * (width + 2 * mesh_rows),
        [
            VM((1, rows), jnp.int32),
            VM((1, rows), jnp.int32),
            VM((rows, width), BF16),
            VM((width, width), BF16),
            VM((1, width), F32),
            VM((2 * mesh_rows, rows), BF16),
            pltpu.SemaphoreType.DMA((4 + rows // ENCODE_BLOCK,)),
        ],
        spaces=[pltpu.HBM] * 5,
    )
    near = to_near(near)
    crossed = swap(cross)
    (sent,) = call(far_kernel, [code, hidden, crossed], [table], 1)
    far = to_far(sent)
    own, sibling = call(
        chip_kernel,
        [sent, code, hidden],
        [((mesh_rows, width), F32), table],
        unit * 2 * mesh_rows,
        spaces=[pl.ANY, VM, VM],
    )
    gather, gather_halo, pick, lead, lead_halo, joined = call(
        prepare_kernel,
        [near, edge_src.T, halo_index.reshape(1, border), proc_out, dec_mesh],
        [
            ((degree * mesh_rows, mesh_rows), BF16),
            ((degree * mesh_rows, 2 * border), BF16),
            ((mesh_rows, border), BF16),
            ((degree * border, mesh_rows), BF16),
            ((degree * border, 2 * border), BF16),
            ((width, width), BF16),
        ],
        LONG,
        spaces=[pl.ANY, VM, VM, VM, VM],
    )
    sibling = swap(sibling)
    latent, halo = call(
        latent_kernel,
        [mesh_feat, own, sibling, near, far, w_enc2, pick],
        [table, border_rows],
        2 * mesh_rows * width * width,
    )
    edge_terms = ((degree * mesh_rows, width), F32)
    for layer in range(L - 1):
        across = to_across(halo)
        before, passed, before_lead = call(
            part(project_kernel, layer),
            [latent, proc_src, proc_dst, proc_bias, gather, halo, lead],
            [edge_terms, border_rows, ((degree * border, width), F32)],
            1,
        )
        beside = swap(passed)
        (across,) = call(pass_kernel, [across], [border_rows], LONG)
        halo, received = call(
            part(lead_kernel, layer),
            [halo, before_lead, across, beside, lead_halo, proc_src, proc_out],
            [border_rows, ((2 * border, width), BF16)],
            2 * border * width * (degree * 2 * border + 3 * width),
        )
        (latent,) = call(
            part(layer_kernel, layer),
            [latent, before, received, gather_halo, proc_out],
            [table],
            1,
        )
    across = to_across(halo)
    before, passed, kept = call(
        part(project_kernel, L - 1),
        [latent, proc_src, proc_dst, proc_bias, gather, halo, dec_mesh],
        [edge_terms, border_rows, ((mesh_rows, width), F32)],
        1,
    )
    beside = swap(passed)
    (across,) = call(pass_kernel, [across], [border_rows], LONG)
    (projected,) = call(
        part(last_layer_kernel, L - 1),
        [before, across, beside, gather_halo, proc_src, kept, joined],
        [table],
        2 * mesh_rows * width * (degree * 2 * border + 2 * width),
    )
    far = to_near(projected)
    f32_rows = ((rows, width), F32)
    pieces = [((mesh_rows // 2, width), BF16)] * 2
    fetch, base, *passed = call(
        base_kernel,
        [code, grid, dec_grid, projected],
        [((rows, 5 * mesh_rows), BF16), f32_rows, *pieces],
        1,
    )
    sibling = [swap(piece) for piece in passed]
    base, passed = call(sibling_kernel, [fetch, base, projected, *sibling], [f32_rows, table], 1)
    near = to_far(passed)
    passed = call(cut_kernel, [far], pieces, 1)
    cross = [swap(piece) for piece in passed]
    (base,) = call(far_add_kernel, [fetch, base, far], [f32_rows], 1)
    (base,) = call(cross_add_kernel, [fetch, base, *cross], [f32_rows], 1)
    tables = [near]
    (out,) = call(
        decode_kernel,
        [fetch, base, *tables, dec_out],
        [((rows, width), BF16)],
        unit * (width + mesh_rows),
        [
            VM((mesh_rows, width), BF16),
            VM((rows, width), BF16),
            pltpu.SemaphoreType.DMA((rows // DECODE_BLOCK,)),
        ],
        out_space=pltpu.HBM,
    )
    return out


def solution(mesh):
    rows = P(("group", "dom", "feat"), None)
    flat = P(("group", "dom", "feat"))
    return jax.shard_map(
        body,
        mesh=mesh,
        in_specs=(rows, rows, rows, flat, flat, rows) + (P(),) * 10,
        out_specs=rows,
        check_vma=False,
    )
```

```python
import functools

import jax
import jax.numpy as jnp
from jax import lax
from jax.experimental import pallas as pl
from jax.experimental.pallas import tpu as pltpu
from jax.sharding import PartitionSpec as P

L = 2
AXES = ("dom", "feat")
F32, BF16 = jnp.float32, jnp.bfloat16
MIB = 1 << 20
BLOCK = 512
ENCODE_BLOCK = 1024
DECODE_BLOCK = 256
LONG = 40_000_000_000


def silu_of_twice(half):
    return half + half * jnp.tanh(half)


def dot(a, b):
    return jnp.dot(a, b, preferred_element_type=F32)


def slot_codes(owner, node, parts, mesh_rows):
    core = lax.axis_index("feat")
    me = lax.axis_index("dom") * 2 + core
    slot = (owner - me) * (1 - 2 * core) + 2
    slot = jnp.where(slot < 0, slot + parts, slot)
    slot = jnp.where(slot >= parts, slot - parts, slot)
    return slot * mesh_rows + node


def one_hot_down(code, first, rows):
    at = lax.broadcasted_iota(jnp.int32, (rows, code.shape[1]), 0)
    return jnp.where(at == code - first, 1.0, 0.0).astype(BF16)


def one_hot_across(row, width):
    n = row.shape[1]
    row = row.astype(F32)
    made = []
    for i in range(0, n, 128):
        cols = jnp.broadcast_to(row[:, i : i + 128], (128, 128)).T
        at = lax.broadcasted_iota(jnp.int32, cols.shape, 1).astype(F32)
        made.append(
            jnp.concatenate(
                [jnp.where(cols == at + float(j), 1.0, 0.0).astype(BF16) for j in range(0, width, 128)],
                axis=1,
            )
        )
    return jnp.concatenate(made, axis=0)


def encode_kernel(parts, owner, node, grid, w1, bias, hidden, near, cross, code, owner_v, node_v, grid_v, w1_v, bias_v, one_hot, sems):
    small = [(owner, owner_v), (node, node_v), (w1, w1_v), (bias, bias_v)]
    copies = [pltpu.make_async_copy(a, b, sems.at[i]) for i, (a, b) in enumerate(small)]
    starts = range(0, grid.shape[0], ENCODE_BLOCK)
    blocks = [
        pltpu.make_async_copy(grid.at[pl.ds(r, ENCODE_BLOCK)], grid_v.at[pl.ds(r, ENCODE_BLOCK)], sems.at[4 + i])
        for i, r in enumerate(starts)
    ]
    for copy in copies + blocks[:1]:
        copy.start()
    copies[0].wait()
    copies[1].wait()
    for copy in blocks[1:]:
        copy.start()
    code[...] = slot_codes(owner_v[...], node_v[...], parts, near.shape[0])
    one_hot[...] = one_hot_down(code[...], 0, one_hot.shape[0])
    copies[2].wait()
    copies[3].wait()
    weights = w1_v[...] * 0.5
    offset = bias_v[...] * 0.5
    for r, copy in zip(starts, blocks):
        copy.wait()
        spot = slice(r, r + ENCODE_BLOCK)
        hidden[spot] = silu_of_twice(dot(grid_v[spot], weights) + offset).astype(BF16)
    rows = near.shape[0]
    cross[...] = dot(one_hot[rows:], hidden[...]).astype(BF16)
    near[...] = dot(one_hot[:rows], hidden[...]).astype(BF16)


def far_kernel(code, hidden, crossed, far):
    rows = far.shape[0]
    far[...] = (dot(one_hot_down(code[...], 4 * rows, rows), hidden[...]) + crossed[...].astype(F32)).astype(BF16)


def chip_kernel(after, code, hidden, own, sibling):
    del after
    rows = own.shape[0]
    sibling[...] = dot(one_hot_down(code[...], 3 * rows, rows), hidden[...]).astype(BF16)
    own[...] = dot(one_hot_down(code[...], 2 * rows, rows), hidden[...])


def prepare_kernel(after, edges, halo_index, w_out, w_mesh, gather, gather_halo, pick, lead, lead_halo, joined):
    del after
    joined[...] = (dot(w_out[L - 1], w_mesh[...]) * 0.5).astype(BF16)
    n, own = edges.shape[1], gather.shape[1]
    border = halo_index.shape[1]
    pick[...] = one_hot_down(halo_index[...], 0, n)
    for k in range(edges.shape[0]):
        one_hot = one_hot_across(edges[k : k + 1, :], own + gather_halo.shape[1])
        gather[k * n : (k + 1) * n] = one_hot[:, :own]
        gather_halo[k * n : (k + 1) * n] = one_hot[:, own:]
        ahead = picked(pick[...], one_hot)
        lead[k * border : (k + 1) * border] = ahead[:, :own]
        lead_halo[k * border : (k + 1) * border] = ahead[:, own:]


def picked(pick, rows):
    return lax.dot_general(pick, rows, (((0,), (0,)), ((), ())), preferred_element_type=F32).astype(BF16)


def latent_kernel(mesh, own, sibling, near, far, w2, pick, latent, halo):
    sums = own[...] + sibling[...].astype(F32) + near[...].astype(F32) + far[...].astype(F32)
    rows = (mesh[...].astype(F32) + dot(sums.astype(BF16), w2[...])).astype(BF16)
    latent[...] = rows
    halo[...] = picked(pick[...], rows)


def own_terms(layer, nodes, gather, source, w_dst, bias, before):
    n = nodes.shape[0]
    target = dot(nodes[...], w_dst[layer]) * 0.5 + bias[layer : layer + 1] * 0.5
    for k in range(gather.shape[0] // n):
        before[k * n : (k + 1) * n] = dot(gather[k * n : (k + 1) * n], source) + target


def project_kernel(layer, latent, w_src, w_dst, bias, gather, halo, more_in, before, passed, more_out):
    source = (dot(latent[...], w_src[layer]) * 0.5).astype(BF16)
    if layer == L - 1:
        more_out[...] = dot(latent[...], more_in[...]) * 0.5
    else:
        own_terms(layer, halo, more_in, source, w_dst, bias, more_out)
    passed[...] = halo[...]
    own_terms(layer, latent, gather, source, w_dst, bias, before)


def halo_table(layer, across, beside, w_src):
    first = lax.axis_index("feat") == 0
    down = jnp.where(first, across[...], beside[...])
    up = jnp.where(first, beside[...], across[...])
    return (dot(jnp.concatenate([down, up], axis=0), w_src[layer]) * 0.5).astype(BF16)


def edge_sums(n, before, gather_halo, table):
    total = None
    for k in range(before.shape[0] // n):
        spot = slice(k * n, (k + 1) * n)
        message = silu_of_twice(dot(gather_halo[spot], table) + before[spot])
        total = message if total is None else total + message
    return total.astype(BF16)


def updated(layer, nodes, before, gather_halo, table, w_out):
    sums = edge_sums(nodes.shape[0], before, gather_halo, table)
    return (nodes[...].astype(F32) + dot(sums, w_out[layer])).astype(BF16)


def lead_kernel(layer, halo, before, across, beside, gather_halo, w_src, w_out, new_halo, table):
    table[...] = halo_table(layer, across, beside, w_src)
    new_halo[...] = updated(layer, halo, before, gather_halo, table[...], w_out)


def layer_kernel(layer, latent, before, table, gather_halo, w_out, new):
    new[...] = updated(layer, latent, before, gather_halo, table[...], w_out)


def last_layer_kernel(layer, before, across, beside, gather_halo, w_src, kept, joined, projected):
    sums = edge_sums(kept.shape[0], before, gather_halo, halo_table(layer, across, beside, w_src))
    projected[...] = (kept[...] + dot(sums, joined[...])).astype(BF16)


def base_kernel(code, grid, w_grid, own, fetch, base, *pieces):
    rows = own.shape[0]
    cut_kernel(own, *pieces)
    for r in range(0, grid.shape[0], BLOCK):
        spot = slice(r, r + BLOCK)
        fetch[spot] = one_hot_across(code[:, spot], fetch.shape[1])
        base[spot] = dot(grid[spot], w_grid[...]) * 0.5 + dot(fetch[spot, 2 * rows : 3 * rows], own[...])


def sibling_kernel(fetch, base, own, *refs):
    *pieces, out, left, right = refs
    rows, half = left.shape
    left[...] = own[:, :half]
    right[...] = own[:, half:]
    table = jnp.concatenate([piece[...] for piece in pieces], axis=0)
    for r in range(0, base.shape[0], BLOCK):
        spot = slice(r, r + BLOCK)
        out[spot] = base[spot] + dot(fetch[spot, 3 * rows : 4 * rows], table)


def far_add_kernel(fetch, base, far, out):
    rows = far.shape[0]
    for r in range(0, base.shape[0], BLOCK):
        spot = slice(r, r + BLOCK)
        out[spot] = base[spot] + dot(fetch[spot, 4 * rows : 5 * rows], far[...])


def cross_add_kernel(fetch, base, *refs):
    *pieces, out = refs
    table = jnp.concatenate([piece[...] for piece in pieces], axis=0)
    rows = table.shape[0]
    for r in range(0, base.shape[0], BLOCK):
        spot = slice(r, r + BLOCK)
        out[spot] = base[spot] + dot(fetch[spot, rows : 2 * rows], table)


def cut_kernel(table, *pieces):
    rows = pieces[0].shape[0]
    for i, piece in enumerate(pieces):
        piece[...] = table[i * rows : (i + 1) * rows]


def pass_kernel(table, out):
    out[...] = table[...]


def ahead_of(block, starts, halved, finish):
    half = halved(0)
    for r in starts:
        ahead = halved(r + block) if r + block <= starts[-1] else None
        finish(r, silu_of_twice(half).astype(BF16))
        half = ahead


def decode_left_kernel(fetch, base, near, w_out, partial):
    rows, width = near.shape
    starts = range(0, base.shape[0], DECODE_BLOCK)

    def halved(r):
        spot = slice(r, r + DECODE_BLOCK)
        return base[spot, :width] + dot(fetch[spot, :rows], near[...])

    def finish(r, hidden):
        partial[r : r + DECODE_BLOCK] = dot(hidden, w_out[:width])

    ahead_of(DECODE_BLOCK, starts, halved, finish)


def decode_kernel(fetch, base, near, w_out, partial, out, out_v, sems):
    rows, width = near.shape
    starts = range(0, base.shape[0], DECODE_BLOCK)
    copies = []

    def halved(r):
        spot = slice(r, r + DECODE_BLOCK)
        return base[spot, width:] + dot(fetch[spot, :rows], near[...])

    def finish(r, hidden):
        spot = slice(r, r + DECODE_BLOCK)
        out_v[spot] = (partial[spot] + dot(hidden, w_out[width:])).astype(BF16)
        place = pl.ds(r, DECODE_BLOCK)
        copies.append(pltpu.make_async_copy(out_v.at[place], out.at[place], sems.at[len(copies)]))
        copies[-1].start()

    ahead_of(DECODE_BLOCK, starts, halved, finish)
    for copy in copies:
        copy.wait()


VM = pltpu.VMEM


def call(kernel, ins, outs, flops, scratch=(), vmem=24, spaces=None, out_space=VM):
    moved = sum(a.size * a.dtype.itemsize for a in ins)
    spaces = spaces or [VM] * len(ins)
    ins = [pltpu.with_memory_space_constraint(a, s) if s is pltpu.HBM else a for a, s in zip(ins, spaces)]
    return pl.pallas_call(
        kernel,
        in_specs=[pl.BlockSpec(memory_space=space) for space in spaces],
        out_specs=[pl.BlockSpec(memory_space=out_space) for _ in outs],
        out_shape=[jax.ShapeDtypeStruct(shape, dtype) for shape, dtype in outs],
        scratch_shapes=list(scratch),
        compiler_params=pltpu.CompilerParams(vmem_limit_bytes=vmem * MIB),
        cost_estimate=pl.CostEstimate(flops=flops, bytes_accessed=moved if flops > 1 else 1, transcendentals=0),
    )(*ins)


def body(
    grid,
    mesh_feat,
    owner,
    node,
    halo_index,
    edge_src,
    w_enc1,
    enc_bias,
    w_enc2,
    proc_src,
    proc_dst,
    proc_bias,
    proc_out,
    dec_grid,
    dec_mesh,
    dec_out,
):
    parts = lax.axis_size(AXES)
    rows, width = grid.shape
    mesh_rows = mesh_feat.shape[0]
    border = halo_index.shape[0]
    degree = edge_src.shape[1]
    part = functools.partial

    def sided(step):
        return [(i, (i + step) % parts if i % 2 == 0 else (i - step) % parts) for i in range(parts)]

    def swap(value):
        return lax.ppermute(value, AXES, sided(1))

    def to_across(value):
        return lax.ppermute(value, AXES, sided(-1))

    def to_near(value):
        return lax.ppermute(value, AXES, sided(-2))

    def to_far(value):
        return lax.ppermute(value, AXES, sided(2))

    table = ((mesh_rows, width), BF16)
    border_rows = ((border, width), BF16)
    unit = 2 * rows * width
    hidden, near, cross, code = call(
        part(encode_kernel, parts),
        [owner.reshape(1, rows), node.reshape(1, rows), grid, w_enc1, enc_bias.reshape(1, width)],
        [((rows, width), BF16), table, table, ((1, rows), jnp.int32)],
        unit * (width + 2 * mesh_rows),
        [
            VM((1, rows), jnp.int32),
            VM((1, rows), jnp.int32),
            VM((rows, width), BF16),
            VM((width, width), BF16),
            VM((1, width), F32),
            VM((2 * mesh_rows, rows), BF16),
            pltpu.SemaphoreType.DMA((4 + rows // ENCODE_BLOCK,)),
        ],
        spaces=[pltpu.HBM] * 5,
    )
    near = to_near(near)
    crossed = swap(cross)
    (sent,) = call(far_kernel, [code, hidden, crossed], [table], 1)
    far = to_far(sent)
    own, sibling = call(
        chip_kernel,
        [sent, code, hidden],
        [((mesh_rows, width), F32), table],
        unit * 2 * mesh_rows,
        spaces=[pl.ANY, VM, VM],
    )
    gather, gather_halo, pick, lead, lead_halo, joined = call(
        prepare_kernel,
        [near, edge_src.T, halo_index.reshape(1, border), proc_out, dec_mesh],
        [
            ((degree * mesh_rows, mesh_rows), BF16),
            ((degree * mesh_rows, 2 * border), BF16),
            ((mesh_rows, border), BF16),
            ((degree * border, mesh_rows), BF16),
            ((degree * border, 2 * border), BF16),
            ((width, width), BF16),
        ],
        LONG,
        spaces=[pl.ANY, VM, VM, VM, VM],
    )
    sibling = swap(sibling)
    latent, halo = call(
        latent_kernel,
        [mesh_feat, own, sibling, near, far, w_enc2, pick],
        [table, border_rows],
        2 * mesh_rows * width * width,
    )
    edge_terms = ((degree * mesh_rows, width), F32)
    for layer in range(L - 1):
        across = to_across(halo)
        before, passed, before_lead = call(
            part(project_kernel, layer),
            [latent, proc_src, proc_dst, proc_bias, gather, halo, lead],
            [edge_terms, border_rows, ((degree * border, width), F32)],
            1,
        )
        beside = swap(passed)
        (across,) = call(pass_kernel, [across], [border_rows], LONG)
        halo, received = call(
            part(lead_kernel, layer),
            [halo, before_lead, across, beside, lead_halo, proc_src, proc_out],
            [border_rows, ((2 * border, width), BF16)],
            2 * border * width * (degree * 2 * border + 3 * width),
        )
        (latent,) = call(
            part(layer_kernel, layer),
            [latent, before, received, gather_halo, proc_out],
            [table],
            1,
        )
    across = to_across(halo)
    before, passed, kept = call(
        part(project_kernel, L - 1),
        [latent, proc_src, proc_dst, proc_bias, gather, halo, dec_mesh],
        [edge_terms, border_rows, ((mesh_rows, width), F32)],
        1,
    )
    beside = swap(passed)
    (across,) = call(pass_kernel, [across], [border_rows], LONG)
    (projected,) = call(
        part(last_layer_kernel, L - 1),
        [before, across, beside, gather_halo, proc_src, kept, joined],
        [table],
        2 * mesh_rows * width * (degree * 2 * border + 2 * width),
    )
    far = to_near(projected)
    f32_rows = ((rows, width), F32)
    pieces = [((mesh_rows // 2, width), BF16)] * 2
    fetch, base, *passed = call(
        base_kernel,
        [code, grid, dec_grid, projected],
        [((rows, 5 * mesh_rows), BF16), f32_rows, *pieces],
        1,
    )
    sibling = [swap(piece) for piece in passed]
    half = ((mesh_rows, width // 2), BF16)
    base, left, right = call(sibling_kernel, [fetch, base, projected, *sibling], [f32_rows, half, half], 1)
    left = to_far(left)
    right = to_far(right)
    passed = call(cut_kernel, [far], [((mesh_rows // 8, width), BF16)] * 8, 1)
    cross = [swap(piece) for piece in passed]
    (base,) = call(far_add_kernel, [fetch, base, far], [f32_rows], 1)
    (base,) = call(cross_add_kernel, [fetch, base, *cross], [f32_rows], 1)
    (partial,) = call(decode_left_kernel, [fetch, base, left, dec_out], [f32_rows], 1)
    (out,) = call(
        decode_kernel,
        [fetch, base, right, dec_out, partial],
        [((rows, width), BF16)],
        unit * (width + mesh_rows),
        [VM((rows, width), BF16), pltpu.SemaphoreType.DMA((rows // DECODE_BLOCK,))],
        out_space=pltpu.HBM,
    )
    return out


def solution(mesh):
    rows = P(("group", "dom", "feat"), None)
    flat = P(("group", "dom", "feat"))
    return jax.shard_map(
        body,
        mesh=mesh,
        in_specs=(rows, rows, rows, flat, flat, rows) + (P(),) * 10,
        out_specs=rows,
        check_vma=False,
    )
```

```python
import functools

import jax
import jax.numpy as jnp
from jax import lax
from jax.experimental import pallas as pl
from jax.experimental.pallas import tpu as pltpu
from jax.sharding import PartitionSpec as P

L = 2
AXES = ("dom", "feat")
F32, BF16 = jnp.float32, jnp.bfloat16
MIB = 1 << 20
BLOCK = 512
ENCODE_BLOCK = 1024
DECODE_BLOCK = 256
LONG = 40_000_000_000


def silu_of_twice(half):
    return half + half * jnp.tanh(half)


def dot(a, b):
    return jnp.dot(a, b, preferred_element_type=F32)


def slot_codes(owner, node, parts, mesh_rows):
    core = lax.axis_index("feat")
    me = lax.axis_index("dom") * 2 + core
    slot = (owner - me) * (1 - 2 * core) + 2
    slot = jnp.where(slot < 0, slot + parts, slot)
    slot = jnp.where(slot >= parts, slot - parts, slot)
    return slot * mesh_rows + node


def one_hot_down(code, first, rows):
    at = lax.broadcasted_iota(jnp.int32, (rows, code.shape[1]), 0)
    return jnp.where(at == code - first, 1.0, 0.0).astype(BF16)


def one_hot_across(row, width):
    n = row.shape[1]
    row = row.astype(F32)
    made = []
    for i in range(0, n, 128):
        cols = jnp.broadcast_to(row[:, i : i + 128], (128, 128)).T
        at = lax.broadcasted_iota(jnp.int32, cols.shape, 1).astype(F32)
        made.append(
            jnp.concatenate(
                [jnp.where(cols == at + float(j), 1.0, 0.0).astype(BF16) for j in range(0, width, 128)],
                axis=1,
            )
        )
    return jnp.concatenate(made, axis=0)


def encode_kernel(parts, owner, node, grid, w1, bias, hidden, near, cross, code, owner_v, node_v, grid_v, w1_v, bias_v, one_hot, sems):
    small = [(owner, owner_v), (node, node_v), (w1, w1_v), (bias, bias_v)]
    copies = [pltpu.make_async_copy(a, b, sems.at[i]) for i, (a, b) in enumerate(small)]
    starts = range(0, grid.shape[0], ENCODE_BLOCK)
    blocks = [
        pltpu.make_async_copy(grid.at[pl.ds(r, ENCODE_BLOCK)], grid_v.at[pl.ds(r, ENCODE_BLOCK)], sems.at[4 + i])
        for i, r in enumerate(starts)
    ]
    for copy in copies + blocks[:1]:
        copy.start()
    copies[0].wait()
    copies[1].wait()
    for copy in blocks[1:]:
        copy.start()
    code[...] = slot_codes(owner_v[...], node_v[...], parts, near.shape[0])
    one_hot[...] = one_hot_down(code[...], 0, one_hot.shape[0])
    copies[2].wait()
    copies[3].wait()
    weights = w1_v[...] * 0.5
    offset = bias_v[...] * 0.5
    for r, copy in zip(starts, blocks):
        copy.wait()
        spot = slice(r, r + ENCODE_BLOCK)
        hidden[spot] = silu_of_twice(dot(grid_v[spot], weights) + offset).astype(BF16)
    rows = near.shape[0]
    cross[...] = dot(one_hot[rows:], hidden[...]).astype(BF16)
    near[...] = dot(one_hot[:rows], hidden[...]).astype(BF16)


def far_kernel(code, hidden, crossed, far):
    rows = far.shape[0]
    far[...] = (dot(one_hot_down(code[...], 4 * rows, rows), hidden[...]) + crossed[...].astype(F32)).astype(BF16)


def chip_kernel(after, code, hidden, halo_index, *refs):
    del after
    held, (own, sibling, pick, joined, kept), buffers, sems = refs[:5], refs[5:10], refs[10:15], refs[15]
    copies = [pltpu.make_async_copy(a, b, sems.at[i]) for i, (a, b) in enumerate(zip(held, buffers))]
    for copy in copies:
        copy.start()
    rows = own.shape[0]
    sibling[...] = dot(one_hot_down(code[...], 3 * rows, rows), hidden[...]).astype(BF16)
    own[...] = dot(one_hot_down(code[...], 2 * rows, rows), hidden[...])
    for copy in copies:
        copy.wait()
    mesh, w2, w_src, w_out, w_mesh = buffers
    pairs = [(w2[...], w_src[0])] + [(w_out[i], w_src[i + 1]) for i in range(L - 1)] + [(w_out[L - 1], w_mesh[...])]
    for i, (first, second) in enumerate(pairs):
        joined[i] = (dot(first, second) * 0.5).astype(BF16)
    pick[...] = one_hot_down(halo_index[...], 0, rows)
    kept[...] = dot(picked(pick[...], mesh[...]), w_src[0]) * 0.5


def prepare_kernel(after, edges, pick, gather, gather_halo, lead, lead_halo):
    del after
    n, own = edges.shape[1], gather.shape[1]
    border = pick.shape[1]
    for k in range(edges.shape[0]):
        one_hot = one_hot_across(edges[k : k + 1, :], own + gather_halo.shape[1])
        gather[k * n : (k + 1) * n] = one_hot[:, :own]
        gather_halo[k * n : (k + 1) * n] = one_hot[:, own:]
        ahead = picked(pick[...], one_hot)
        lead[k * border : (k + 1) * border] = ahead[:, :own]
        lead_halo[k * border : (k + 1) * border] = ahead[:, own:]


def picked(pick, rows):
    return lax.dot_general(pick, rows, (((0,), (0,)), ((), ())), preferred_element_type=F32).astype(BF16)


def sums_kernel(after, own, sibling, near, far, pick, joined, kept, sums, halo):
    del after
    total = own[...] + sibling[...].astype(F32) + near[...].astype(F32) + far[...].astype(F32)
    sums[...] = total.astype(BF16)
    halo[...] = (kept[...] + dot(picked(pick[...], sums[...]), joined[0])).astype(BF16)


def latent_kernel(mesh, sums, w2, latent):
    latent[...] = (mesh[...].astype(F32) + dot(sums[...], w2[...])).astype(BF16)


def own_terms(layer, nodes, gather, source, w_dst, bias, before):
    n = nodes.shape[0]
    target = dot(nodes[...], w_dst[layer]) * 0.5 + bias[layer : layer + 1] * 0.5
    for k in range(gather.shape[0] // n):
        before[k * n : (k + 1) * n] = dot(gather[k * n : (k + 1) * n], source) + target


def project_kernel(layer, latent, w_src, w_dst, bias, gather, halo, w_next, *refs):
    source = (dot(latent[...], w_src[layer]) * 0.5).astype(BF16)
    if layer == L - 1:
        before, passed, kept = refs
        kept[...] = dot(latent[...], w_next[...]) * 0.5
    else:
        pick, lead, before, passed, kept, before_lead = refs
        nodes = picked(pick[...], latent[...])
        kept[...] = dot(nodes, w_next[layer + 1]) * 0.5
        own_terms(layer, nodes, lead, source, w_dst, bias, before_lead)
    passed[...] = halo[...]
    own_terms(layer, latent, gather, source, w_dst, bias, before)


def halo_table(across, beside):
    first = lax.axis_index("feat") == 0
    down = jnp.where(first, across[...], beside[...])
    up = jnp.where(first, beside[...], across[...])
    return jnp.concatenate([down, up], axis=0)


def edge_sums(n, before, gather_halo, table):
    total = None
    for k in range(before.shape[0] // n):
        spot = slice(k * n, (k + 1) * n)
        message = silu_of_twice(dot(gather_halo[spot], table) + before[spot])
        total = message if total is None else total + message
    return total.astype(BF16)


def lead_kernel(layer, before, across, beside, gather_halo, joined, kept, halo):
    sums = edge_sums(kept.shape[0], before, gather_halo, halo_table(across, beside))
    halo[...] = (kept[...] + dot(sums, joined[layer + 1])).astype(BF16)


def layer_kernel(layer, latent, before, across, beside, gather_halo, w_out, new):
    sums = edge_sums(latent.shape[0], before, gather_halo, halo_table(across, beside))
    new[...] = (latent[...].astype(F32) + dot(sums, w_out[layer])).astype(BF16)


def last_layer_kernel(before, across, beside, gather_halo, kept, joined, projected):
    sums = edge_sums(kept.shape[0], before, gather_halo, halo_table(across, beside))
    projected[...] = (kept[...] + dot(sums, joined[L])).astype(BF16)


def base_kernel(code, grid, w_grid, own, fetch, base, *pieces):
    rows = own.shape[0]
    cut_kernel(own, *pieces)
    for r in range(0, grid.shape[0], BLOCK):
        spot = slice(r, r + BLOCK)
        fetch[spot] = one_hot_across(code[:, spot], fetch.shape[1])
        base[spot] = dot(grid[spot], w_grid[...]) * 0.5 + dot(fetch[spot, 2 * rows : 3 * rows], own[...])


def sibling_kernel(fetch, base, own, *refs):
    *pieces, out, left, right = refs
    rows, half = left.shape
    left[...] = own[:, :half]
    right[...] = own[:, half:]
    table = jnp.concatenate([piece[...] for piece in pieces], axis=0)
    for r in range(0, base.shape[0], BLOCK):
        spot = slice(r, r + BLOCK)
        out[spot] = base[spot] + dot(fetch[spot, 3 * rows : 4 * rows], table)


def far_add_kernel(fetch, base, far, out):
    rows = far.shape[0]
    for r in range(0, base.shape[0], BLOCK):
        spot = slice(r, r + BLOCK)
        out[spot] = base[spot] + dot(fetch[spot, 4 * rows : 5 * rows], far[...])


def cross_add_kernel(fetch, base, *refs):
    *pieces, out = refs
    table = jnp.concatenate([piece[...] for piece in pieces], axis=0)
    rows = table.shape[0]
    for r in range(0, base.shape[0], BLOCK):
        spot = slice(r, r + BLOCK)
        out[spot] = base[spot] + dot(fetch[spot, rows : 2 * rows], table)


def cut_kernel(table, *pieces):
    row = column = 0
    for piece in pieces:
        rows, width = piece.shape
        piece[...] = table[row : row + rows, column : column + width]
        row += rows
        if row == table.shape[0]:
            row, column = 0, column + width


def pass_kernel(table, out):
    out[...] = table[...]


def ahead_of(block, starts, halved, finish):
    half = halved(0)
    for r in starts:
        ahead = halved(r + block) if r + block <= starts[-1] else None
        finish(r, silu_of_twice(half).astype(BF16))
        half = ahead


def decode_left_kernel(fetch, base, near, w_out, partial):
    rows, width = near.shape
    starts = range(0, base.shape[0], DECODE_BLOCK)

    def halved(r):
        spot = slice(r, r + DECODE_BLOCK)
        return base[spot, :width] + dot(fetch[spot, :rows], near[...])

    def finish(r, hidden):
        partial[r : r + DECODE_BLOCK] = dot(hidden, w_out[:width])

    ahead_of(DECODE_BLOCK, starts, halved, finish)


def decode_kernel(fetch, base, near, w_out, partial, out, out_v, sems):
    rows, width = near.shape
    starts = range(0, base.shape[0], DECODE_BLOCK)
    copies = []

    def halved(r):
        spot = slice(r, r + DECODE_BLOCK)
        return base[spot, width:] + dot(fetch[spot, :rows], near[...])

    def finish(r, hidden):
        spot = slice(r, r + DECODE_BLOCK)
        out_v[spot] = (partial[spot] + dot(hidden, w_out[width:])).astype(BF16)
        place = pl.ds(r, DECODE_BLOCK)
        copies.append(pltpu.make_async_copy(out_v.at[place], out.at[place], sems.at[len(copies)]))
        copies[-1].start()

    ahead_of(DECODE_BLOCK, starts, halved, finish)
    for copy in copies:
        copy.wait()


VM = pltpu.VMEM


def call(kernel, ins, outs, flops, scratch=(), vmem=24, spaces=None, out_space=VM):
    moved = sum(a.size * a.dtype.itemsize for a in ins)
    spaces = spaces or [VM] * len(ins)
    ins = [pltpu.with_memory_space_constraint(a, s) if s is pltpu.HBM else a for a, s in zip(ins, spaces)]
    return pl.pallas_call(
        kernel,
        in_specs=[pl.BlockSpec(memory_space=space) for space in spaces],
        out_specs=[pl.BlockSpec(memory_space=out_space) for _ in outs],
        out_shape=[jax.ShapeDtypeStruct(shape, dtype) for shape, dtype in outs],
        scratch_shapes=list(scratch),
        compiler_params=pltpu.CompilerParams(vmem_limit_bytes=vmem * MIB),
        cost_estimate=pl.CostEstimate(flops=flops, bytes_accessed=moved if flops > 1 else 1, transcendentals=0),
    )(*ins)


def body(
    grid,
    mesh_feat,
    owner,
    node,
    halo_index,
    edge_src,
    w_enc1,
    enc_bias,
    w_enc2,
    proc_src,
    proc_dst,
    proc_bias,
    proc_out,
    dec_grid,
    dec_mesh,
    dec_out,
):
    parts = lax.axis_size(AXES)
    rows, width = grid.shape
    mesh_rows = mesh_feat.shape[0]
    border = halo_index.shape[0]
    degree = edge_src.shape[1]
    part = functools.partial

    def sided(step):
        return [(i, (i + step) % parts if i % 2 == 0 else (i - step) % parts) for i in range(parts)]

    def swap(value):
        return lax.ppermute(value, AXES, sided(1))

    def to_across(value):
        return lax.ppermute(value, AXES, sided(-1))

    def to_near(value):
        return lax.ppermute(value, AXES, sided(-2))

    def to_far(value):
        return lax.ppermute(value, AXES, sided(2))

    table = ((mesh_rows, width), BF16)
    border_rows = ((border, width), BF16)
    unit = 2 * rows * width
    hidden, near, cross, code = call(
        part(encode_kernel, parts),
        [owner.reshape(1, rows), node.reshape(1, rows), grid, w_enc1, enc_bias.reshape(1, width)],
        [((rows, width), BF16), table, table, ((1, rows), jnp.int32)],
        unit * (width + 2 * mesh_rows),
        [
            VM((1, rows), jnp.int32),
            VM((1, rows), jnp.int32),
            VM((rows, width), BF16),
            VM((width, width), BF16),
            VM((1, width), F32),
            VM((2 * mesh_rows, rows), BF16),
            pltpu.SemaphoreType.DMA((4 + rows // ENCODE_BLOCK,)),
        ],
        spaces=[pltpu.HBM] * 5,
    )
    near = to_near(near)
    crossed = swap(cross)
    (sent,) = call(far_kernel, [code, hidden, crossed], [table], 1)
    far = to_far(sent)
    own, sibling, pick, joined, kept = call(
        chip_kernel,
        [sent, code, hidden, halo_index.reshape(1, border), mesh_feat, w_enc2, proc_src, proc_out, dec_mesh],
        [
            ((mesh_rows, width), F32),
            table,
            ((mesh_rows, border), BF16),
            ((L + 1, width, width), BF16),
            ((border, width), F32),
        ],
        unit * 2 * mesh_rows,
        [
            VM((mesh_rows, width), BF16),
            VM((width, width), BF16),
            VM((L, width, width), BF16),
            VM((L, width, width), BF16),
            VM((width, width), BF16),
            pltpu.SemaphoreType.DMA((5,)),
        ],
        spaces=[pl.ANY] + [VM] * 3 + [pltpu.HBM] * 5,
    )
    gather, gather_halo, lead, lead_halo = call(
        prepare_kernel,
        [near, edge_src.T, pick],
        [
            ((degree * mesh_rows, mesh_rows), BF16),
            ((degree * mesh_rows, 2 * border), BF16),
            ((degree * border, mesh_rows), BF16),
            ((degree * border, 2 * border), BF16),
        ],
        LONG,
        spaces=[pl.ANY, VM, VM],
    )
    sibling = swap(sibling)
    sums, halo = call(
        sums_kernel,
        [lead_halo, own, sibling, near, far, pick, joined, kept],
        [table, border_rows],
        2 * mesh_rows * width * width,
        spaces=[pl.ANY] + [VM] * 7,
    )
    across = to_across(halo)
    (latent,) = call(latent_kernel, [mesh_feat, sums, w_enc2], [table], 1)
    edge_terms = ((degree * mesh_rows, width), F32)
    for layer in range(L - 1):
        before, passed, kept, before_lead = call(
            part(project_kernel, layer),
            [latent, proc_src, proc_dst, proc_bias, gather, halo, proc_src, pick, lead],
            [edge_terms, border_rows, ((border, width), F32), ((degree * border, width), F32)],
            1,
        )
        beside = swap(passed)
        (across,) = call(pass_kernel, [across], [border_rows], LONG)
        (halo,) = call(
            part(lead_kernel, layer),
            [before_lead, across, beside, lead_halo, joined, kept],
            [border_rows],
            2 * border * width * (degree * 2 * border + 3 * width),
        )
        arrived = (across, beside)
        across = to_across(halo)
        (latent,) = call(
            part(layer_kernel, layer),
            [latent, before, *arrived, gather_halo, proc_out],
            [table],
            1,
        )
    before, passed, kept = call(
        part(project_kernel, L - 1),
        [latent, proc_src, proc_dst, proc_bias, gather, halo, dec_mesh],
        [edge_terms, border_rows, ((mesh_rows, width), F32)],
        1,
    )
    beside = swap(passed)
    (across,) = call(pass_kernel, [across], [border_rows], LONG)
    (projected,) = call(
        last_layer_kernel,
        [before, across, beside, gather_halo, kept, joined],
        [table],
        2 * mesh_rows * width * (degree * 2 * border + 2 * width),
    )
    far = to_near(projected)
    f32_rows = ((rows, width), F32)
    pieces = [((mesh_rows // 2, width), BF16)] * 2
    fetch, base, *passed = call(
        base_kernel,
        [code, grid, dec_grid, projected],
        [((rows, 5 * mesh_rows), BF16), f32_rows, *pieces],
        1,
    )
    sibling = [swap(piece) for piece in passed]
    half = ((mesh_rows, width // 2), BF16)
    base, left, right = call(sibling_kernel, [fetch, base, projected, *sibling], [f32_rows, half, half], 1)
    left = to_far(left)
    right = to_far(right)
    passed = call(cut_kernel, [far], [((mesh_rows * part_rows // 256, width), BF16) for part_rows in (48, 48, 48, 48, 32, 32)], 1)
    cross = [swap(piece) for piece in passed]
    (base,) = call(far_add_kernel, [fetch, base, far], [f32_rows], 1)
    (base,) = call(cross_add_kernel, [fetch, base, *cross], [f32_rows], 1)
    (partial,) = call(decode_left_kernel, [fetch, base, left, dec_out], [f32_rows], 1)
    (out,) = call(
        decode_kernel,
        [fetch, base, right, dec_out, partial],
        [((rows, width), BF16)],
        unit * (width + mesh_rows),
        [VM((rows, width), BF16), pltpu.SemaphoreType.DMA((rows // DECODE_BLOCK,))],
        out_space=pltpu.HBM,
    )
    return out


def solution(mesh):
    rows = P(("group", "dom", "feat"), None)
    flat = P(("group", "dom", "feat"))
    return jax.shard_map(
        body,
        mesh=mesh,
        in_specs=(rows, rows, rows, flat, flat, rows) + (P(),) * 10,
        out_specs=rows,
        check_vma=False,
    )
```

```python
import functools

import jax
import jax.numpy as jnp
from jax import lax
from jax.experimental import pallas as pl
from jax.experimental.pallas import tpu as pltpu
from jax.sharding import PartitionSpec as P

L = 2
AXES = ("dom", "feat")
F32, BF16 = jnp.float32, jnp.bfloat16
MIB = 1 << 20
BLOCK = 512
ENCODE_BLOCK = 1024
DECODE_BLOCK = 256
LONG = 40_000_000_000


def silu_of_twice(half):
    return half + half * jnp.tanh(half)


def dot(a, b):
    return jnp.dot(a, b, preferred_element_type=F32)


def slot_codes(owner, node, parts, mesh_rows):
    core = lax.axis_index("feat")
    me = lax.axis_index("dom") * 2 + core
    slot = (owner - me) * (1 - 2 * core) + 2
    slot = jnp.where(slot < 0, slot + parts, slot)
    slot = jnp.where(slot >= parts, slot - parts, slot)
    return slot * mesh_rows + node


def one_hot_down(code, first, rows):
    at = lax.broadcasted_iota(jnp.int32, (rows, code.shape[1]), 0)
    return jnp.where(at == code - first, 1.0, 0.0).astype(BF16)


def one_hot_across(row, width):
    n = row.shape[1]
    row = row.astype(F32)
    made = []
    for i in range(0, n, 128):
        cols = jnp.broadcast_to(row[:, i : i + 128], (128, 128)).T
        at = lax.broadcasted_iota(jnp.int32, cols.shape, 1).astype(F32)
        made.append(
            jnp.concatenate(
                [jnp.where(cols == at + float(j), 1.0, 0.0).astype(BF16) for j in range(0, width, 128)],
                axis=1,
            )
        )
    return jnp.concatenate(made, axis=0)


def encode_kernel(parts, owner, node, grid, w1, bias, hidden, near, cross, code, owner_v, node_v, grid_v, w1_v, bias_v, one_hot, sems):
    small = [(owner, owner_v), (node, node_v), (w1, w1_v), (bias, bias_v)]
    copies = [pltpu.make_async_copy(a, b, sems.at[i]) for i, (a, b) in enumerate(small)]
    starts = range(0, grid.shape[0], ENCODE_BLOCK)
    blocks = [
        pltpu.make_async_copy(grid.at[pl.ds(r, ENCODE_BLOCK)], grid_v.at[pl.ds(r, ENCODE_BLOCK)], sems.at[4 + i])
        for i, r in enumerate(starts)
    ]
    for copy in copies + blocks[:1]:
        copy.start()
    copies[0].wait()
    copies[1].wait()
    for copy in blocks[1:]:
        copy.start()
    code[...] = slot_codes(owner_v[...], node_v[...], parts, near.shape[0])
    one_hot[...] = one_hot_down(code[...], 0, one_hot.shape[0])
    copies[2].wait()
    copies[3].wait()
    weights = w1_v[...] * 0.5
    offset = bias_v[...] * 0.5
    for r, copy in zip(starts, blocks):
        copy.wait()
        spot = slice(r, r + ENCODE_BLOCK)
        hidden[spot] = silu_of_twice(dot(grid_v[spot], weights) + offset).astype(BF16)
    rows = near.shape[0]
    cross[...] = dot(one_hot[rows:], hidden[...]).astype(BF16)
    near[...] = dot(one_hot[:rows], hidden[...]).astype(BF16)


def far_kernel(code, hidden, crossed, far):
    rows = far.shape[0]
    far[...] = (dot(one_hot_down(code[...], 4 * rows, rows), hidden[...]) + crossed[...].astype(F32)).astype(BF16)


def chip_kernel(after, code, hidden, halo_index, *refs):
    del after
    held, (own, sibling, pick, joined, kept, fetch), buffers, sems = refs[:5], refs[5:11], refs[11:16], refs[16]
    copies = [pltpu.make_async_copy(a, b, sems.at[i]) for i, (a, b) in enumerate(zip(held, buffers))]
    for copy in copies:
        copy.start()
    rows = own.shape[0]
    sibling[...] = dot(one_hot_down(code[...], 3 * rows, rows), hidden[...]).astype(BF16)
    own[...] = dot(one_hot_down(code[...], 2 * rows, rows), hidden[...])
    for r in range(0, fetch.shape[0], BLOCK):
        fetch[r : r + BLOCK] = one_hot_across(code[:, r : r + BLOCK], fetch.shape[1])
    for copy in copies:
        copy.wait()
    mesh, w2, w_src, w_out, w_mesh = buffers
    pairs = [(w2[...], w_src[0])] + [(w_out[i], w_src[i + 1]) for i in range(L - 1)] + [(w_out[L - 1], w_mesh[...])]
    for i, (first, second) in enumerate(pairs):
        joined[i] = (dot(first, second) * 0.5).astype(BF16)
    pick[...] = one_hot_down(halo_index[...], 0, rows)
    kept[...] = dot(picked(pick[...], mesh[...]), w_src[0]) * 0.5


def prepare_kernel(after, edges, pick, gather, gather_halo, lead, lead_halo):
    del after
    n, own = edges.shape[1], gather.shape[1]
    border = pick.shape[1]
    for k in range(edges.shape[0]):
        one_hot = one_hot_across(edges[k : k + 1, :], own + gather_halo.shape[1])
        gather[k * n : (k + 1) * n] = one_hot[:, :own]
        gather_halo[k * n : (k + 1) * n] = one_hot[:, own:]
        ahead = picked(pick[...], one_hot)
        lead[k * border : (k + 1) * border] = ahead[:, :own]
        lead_halo[k * border : (k + 1) * border] = ahead[:, own:]


def picked(pick, rows):
    return lax.dot_general(pick, rows, (((0,), (0,)), ((), ())), preferred_element_type=F32).astype(BF16)


def sums_kernel(after, own, sibling, near, far, pick, joined, kept, sums, halo):
    del after
    total = own[...] + sibling[...].astype(F32) + near[...].astype(F32) + far[...].astype(F32)
    sums[...] = total.astype(BF16)
    halo[...] = (kept[...] + dot(picked(pick[...], sums[...]), joined[0])).astype(BF16)


def latent_kernel(mesh, sums, w2, latent):
    latent[...] = (mesh[...].astype(F32) + dot(sums[...], w2[...])).astype(BF16)


def own_terms(layer, nodes, gather, source, w_dst, bias, before):
    n = nodes.shape[0]
    target = dot(nodes[...], w_dst[layer]) * 0.5 + bias[layer : layer + 1] * 0.5
    for k in range(gather.shape[0] // n):
        before[k * n : (k + 1) * n] = dot(gather[k * n : (k + 1) * n], source) + target


def project_kernel(layer, latent, w_src, w_dst, bias, gather, halo, w_next, *refs):
    source = (dot(latent[...], w_src[layer]) * 0.5).astype(BF16)
    if layer == L - 1:
        before, passed, kept = refs
        kept[...] = dot(latent[...], w_next[...]) * 0.5
    else:
        pick, lead, before, passed, kept, before_lead = refs
        nodes = picked(pick[...], latent[...])
        kept[...] = dot(nodes, w_next[layer + 1]) * 0.5
        own_terms(layer, nodes, lead, source, w_dst, bias, before_lead)
    passed[...] = halo[...]
    own_terms(layer, latent, gather, source, w_dst, bias, before)


def halo_table(across, beside):
    first = lax.axis_index("feat") == 0
    down = jnp.where(first, across[...], beside[...])
    up = jnp.where(first, beside[...], across[...])
    return jnp.concatenate([down, up], axis=0)


def edge_sums(n, before, gather_halo, table):
    total = None
    for k in range(before.shape[0] // n):
        spot = slice(k * n, (k + 1) * n)
        message = silu_of_twice(dot(gather_halo[spot], table) + before[spot])
        total = message if total is None else total + message
    return total.astype(BF16)


def lead_kernel(layer, before, across, beside, gather_halo, joined, kept, halo):
    sums = edge_sums(kept.shape[0], before, gather_halo, halo_table(across, beside))
    halo[...] = (kept[...] + dot(sums, joined[layer + 1])).astype(BF16)


def layer_kernel(layer, latent, before, across, beside, gather_halo, w_out, new):
    sums = edge_sums(latent.shape[0], before, gather_halo, halo_table(across, beside))
    new[...] = (latent[...].astype(F32) + dot(sums, w_out[layer])).astype(BF16)


def last_layer_kernel(before, across, beside, gather_halo, kept, joined, projected):
    sums = edge_sums(kept.shape[0], before, gather_halo, halo_table(across, beside))
    projected[...] = (kept[...] + dot(sums, joined[L])).astype(BF16)


def base_kernel(grid, w_grid, fetch, own, base, *pieces):
    rows = own.shape[0]
    cut_kernel(own, *pieces)
    for r in range(0, grid.shape[0], BLOCK):
        spot = slice(r, r + BLOCK)
        base[spot] = dot(grid[spot], w_grid[...]) * 0.5 + dot(fetch[spot, 2 * rows : 3 * rows], own[...])


def sibling_kernel(fetch, base, own, *refs):
    *pieces, out, left, right = refs
    rows, half = left.shape
    left[...] = own[:, :half]
    right[...] = own[:, half:]
    table = jnp.concatenate([piece[...] for piece in pieces], axis=0)
    for r in range(0, base.shape[0], BLOCK):
        spot = slice(r, r + BLOCK)
        out[spot] = base[spot] + dot(fetch[spot, 3 * rows : 4 * rows], table)


def far_add_kernel(fetch, base, far, out):
    rows = far.shape[0]
    for r in range(0, base.shape[0], BLOCK):
        spot = slice(r, r + BLOCK)
        out[spot] = base[spot] + dot(fetch[spot, 4 * rows : 5 * rows], far[...])


def cross_add_kernel(fetch, base, *refs):
    *pieces, out = refs
    table = jnp.concatenate([piece[...] for piece in pieces], axis=0)
    rows = table.shape[0]
    for r in range(0, base.shape[0], BLOCK):
        spot = slice(r, r + BLOCK)
        out[spot] = base[spot] + dot(fetch[spot, rows : 2 * rows], table)


def cut_kernel(table, *pieces):
    row = column = 0
    for piece in pieces:
        rows, width = piece.shape
        piece[...] = table[row : row + rows, column : column + width]
        row += rows
        if row == table.shape[0]:
            row, column = 0, column + width


def pass_kernel(table, out):
    out[...] = table[...]


def ahead_of(block, starts, halved, finish):
    half = halved(0)
    for r in starts:
        ahead = halved(r + block) if r + block <= starts[-1] else None
        finish(r, silu_of_twice(half).astype(BF16))
        half = ahead


def decode_left_kernel(fetch, base, near, w_out, partial):
    rows, width = near.shape
    starts = range(0, base.shape[0], DECODE_BLOCK)

    def halved(r):
        spot = slice(r, r + DECODE_BLOCK)
        return base[spot, :width] + dot(fetch[spot, :rows], near[...])

    def finish(r, hidden):
        partial[r : r + DECODE_BLOCK] = dot(hidden, w_out[:width])

    ahead_of(DECODE_BLOCK, starts, halved, finish)


def decode_kernel(fetch, base, near, w_out, partial, out, out_v, sems):
    rows, width = near.shape
    starts = range(0, base.shape[0], DECODE_BLOCK)
    copies = []

    def halved(r):
        spot = slice(r, r + DECODE_BLOCK)
        return base[spot, width:] + dot(fetch[spot, :rows], near[...])

    def finish(r, hidden):
        spot = slice(r, r + DECODE_BLOCK)
        out_v[spot] = (partial[spot] + dot(hidden, w_out[width:])).astype(BF16)
        place = pl.ds(r, DECODE_BLOCK)
        copies.append(pltpu.make_async_copy(out_v.at[place], out.at[place], sems.at[len(copies)]))
        copies[-1].start()

    ahead_of(DECODE_BLOCK, starts, halved, finish)
    for copy in copies:
        copy.wait()


VM = pltpu.VMEM


def call(kernel, ins, outs, flops, scratch=(), vmem=24, spaces=None, out_space=VM):
    moved = sum(a.size * a.dtype.itemsize for a in ins)
    spaces = spaces or [VM] * len(ins)
    ins = [pltpu.with_memory_space_constraint(a, s) if s is pltpu.HBM else a for a, s in zip(ins, spaces)]
    return pl.pallas_call(
        kernel,
        in_specs=[pl.BlockSpec(memory_space=space) for space in spaces],
        out_specs=[pl.BlockSpec(memory_space=out_space) for _ in outs],
        out_shape=[jax.ShapeDtypeStruct(shape, dtype) for shape, dtype in outs],
        scratch_shapes=list(scratch),
        compiler_params=pltpu.CompilerParams(vmem_limit_bytes=vmem * MIB),
        cost_estimate=pl.CostEstimate(flops=flops, bytes_accessed=moved if flops > 1 else 1, transcendentals=0),
    )(*ins)


def body(
    grid,
    mesh_feat,
    owner,
    node,
    halo_index,
    edge_src,
    w_enc1,
    enc_bias,
    w_enc2,
    proc_src,
    proc_dst,
    proc_bias,
    proc_out,
    dec_grid,
    dec_mesh,
    dec_out,
):
    parts = lax.axis_size(AXES)
    rows, width = grid.shape
    mesh_rows = mesh_feat.shape[0]
    border = halo_index.shape[0]
    degree = edge_src.shape[1]
    part = functools.partial

    def sided(step):
        return [(i, (i + step) % parts if i % 2 == 0 else (i - step) % parts) for i in range(parts)]

    def swap(value):
        return lax.ppermute(value, AXES, sided(1))

    def to_across(value):
        return lax.ppermute(value, AXES, sided(-1))

    def to_near(value):
        return lax.ppermute(value, AXES, sided(-2))

    def to_far(value):
        return lax.ppermute(value, AXES, sided(2))

    table = ((mesh_rows, width), BF16)
    border_rows = ((border, width), BF16)
    unit = 2 * rows * width
    hidden, near, cross, code = call(
        part(encode_kernel, parts),
        [owner.reshape(1, rows), node.reshape(1, rows), grid, w_enc1, enc_bias.reshape(1, width)],
        [((rows, width), BF16), table, table, ((1, rows), jnp.int32)],
        unit * (width + 2 * mesh_rows),
        [
            VM((1, rows), jnp.int32),
            VM((1, rows), jnp.int32),
            VM((rows, width), BF16),
            VM((width, width), BF16),
            VM((1, width), F32),
            VM((2 * mesh_rows, rows), BF16),
            pltpu.SemaphoreType.DMA((4 + rows // ENCODE_BLOCK,)),
        ],
        spaces=[pltpu.HBM] * 5,
    )
    near = to_near(near)
    crossed = swap(cross)
    (sent,) = call(far_kernel, [code, hidden, crossed], [table], 1)
    far = to_far(sent)
    own, sibling, pick, joined, kept, fetch = call(
        chip_kernel,
        [sent, code, hidden, halo_index.reshape(1, border), mesh_feat, w_enc2, proc_src, proc_out, dec_mesh],
        [
            ((mesh_rows, width), F32),
            table,
            ((mesh_rows, border), BF16),
            ((L + 1, width, width), BF16),
            ((border, width), F32),
            ((rows, 5 * mesh_rows), BF16),
        ],
        unit * 2 * mesh_rows,
        [
            VM((mesh_rows, width), BF16),
            VM((width, width), BF16),
            VM((L, width, width), BF16),
            VM((L, width, width), BF16),
            VM((width, width), BF16),
            pltpu.SemaphoreType.DMA((5,)),
        ],
        spaces=[pl.ANY] + [VM] * 3 + [pltpu.HBM] * 5,
    )
    gather, gather_halo, lead, lead_halo = call(
        prepare_kernel,
        [near, edge_src.T, pick],
        [
            ((degree * mesh_rows, mesh_rows), BF16),
            ((degree * mesh_rows, 2 * border), BF16),
            ((degree * border, mesh_rows), BF16),
            ((degree * border, 2 * border), BF16),
        ],
        LONG,
        spaces=[pl.ANY, VM, VM],
    )
    sibling = swap(sibling)
    sums, halo = call(
        sums_kernel,
        [lead_halo, own, sibling, near, far, pick, joined, kept],
        [table, border_rows],
        2 * mesh_rows * width * width,
        spaces=[pl.ANY] + [VM] * 7,
    )
    across = to_across(halo)
    (latent,) = call(latent_kernel, [mesh_feat, sums, w_enc2], [table], 1)
    edge_terms = ((degree * mesh_rows, width), F32)
    for layer in range(L - 1):
        before, passed, kept, before_lead = call(
            part(project_kernel, layer),
            [latent, proc_src, proc_dst, proc_bias, gather, halo, proc_src, pick, lead],
            [edge_terms, border_rows, ((border, width), F32), ((degree * border, width), F32)],
            1,
        )
        beside = swap(passed)
        (across,) = call(pass_kernel, [across], [border_rows], LONG)
        (halo,) = call(
            part(lead_kernel, layer),
            [before_lead, across, beside, lead_halo, joined, kept],
            [border_rows],
            2 * border * width * (degree * 2 * border + 3 * width),
        )
        arrived = (across, beside)
        across = to_across(halo)
        (latent,) = call(
            part(layer_kernel, layer),
            [latent, before, *arrived, gather_halo, proc_out],
            [table],
            1,
        )
    before, passed, kept = call(
        part(project_kernel, L - 1),
        [latent, proc_src, proc_dst, proc_bias, gather, halo, dec_mesh],
        [edge_terms, border_rows, ((mesh_rows, width), F32)],
        1,
    )
    beside = swap(passed)
    (across,) = call(pass_kernel, [across], [border_rows], LONG)
    (projected,) = call(
        last_layer_kernel,
        [before, across, beside, gather_halo, kept, joined],
        [table],
        2 * mesh_rows * width * (degree * 2 * border + 2 * width),
    )
    far = to_near(projected)
    f32_rows = ((rows, width), F32)
    pieces = [((mesh_rows // 2, width), BF16)] * 2
    base, *passed = call(
        base_kernel,
        [grid, dec_grid, fetch, projected],
        [f32_rows, *pieces],
        1,
    )
    sibling = [swap(piece) for piece in passed]
    half = ((mesh_rows, width // 2), BF16)
    base, left, right = call(sibling_kernel, [fetch, base, projected, *sibling], [f32_rows, half, half], 1)
    left = to_far(left)
    right = to_far(right)
    passed = call(cut_kernel, [far], [((mesh_rows * part_rows // 256, width), BF16) for part_rows in (64, 48, 48, 48, 48)], 1)
    cross = [swap(piece) for piece in passed]
    (base,) = call(far_add_kernel, [fetch, base, far], [f32_rows], 1)
    (base,) = call(cross_add_kernel, [fetch, base, *cross], [f32_rows], 1)
    (partial,) = call(decode_left_kernel, [fetch, base, left, dec_out], [f32_rows], 1)
    (out,) = call(
        decode_kernel,
        [fetch, base, right, dec_out, partial],
        [((rows, width), BF16)],
        unit * (width + mesh_rows),
        [VM((rows, width), BF16), pltpu.SemaphoreType.DMA((rows // DECODE_BLOCK,))],
        out_space=pltpu.HBM,
    )
    return out


def solution(mesh):
    rows = P(("group", "dom", "feat"), None)
    flat = P(("group", "dom", "feat"))
    return jax.shard_map(
        body,
        mesh=mesh,
        in_specs=(rows, rows, rows, flat, flat, rows) + (P(),) * 10,
        out_specs=rows,
        check_vma=False,
    )
```

```python
import functools

import jax
import jax.numpy as jnp
from jax import lax
from jax.experimental import pallas as pl
from jax.experimental.pallas import tpu as pltpu
from jax.sharding import PartitionSpec as P

L = 2
AXES = ("dom", "feat")
F32, BF16 = jnp.float32, jnp.bfloat16
MIB = 1 << 20
BLOCK = 512
ENCODE_BLOCK = 1024
DECODE_BLOCK = 256
LONG = 40_000_000_000


def silu_of_twice(half):
    return half + half * jnp.tanh(half)


def dot(a, b):
    return jnp.dot(a, b, preferred_element_type=F32)


def slot_codes(owner, node, parts, mesh_rows):
    core = lax.axis_index("feat")
    me = lax.axis_index("dom") * 2 + core
    slot = (owner - me) * (1 - 2 * core) + 2
    slot = jnp.where(slot < 0, slot + parts, slot)
    slot = jnp.where(slot >= parts, slot - parts, slot)
    return slot * mesh_rows + node


def one_hot_down(code, first, rows):
    at = lax.broadcasted_iota(jnp.int32, (rows, code.shape[1]), 0)
    return jnp.where(at == code - first, 1.0, 0.0).astype(BF16)


def one_hot_across(row, width):
    n = row.shape[1]
    row = row.astype(F32)
    made = []
    for i in range(0, n, 128):
        cols = jnp.broadcast_to(row[:, i : i + 128], (128, 128)).T
        at = lax.broadcasted_iota(jnp.int32, cols.shape, 1).astype(F32)
        made.append(
            jnp.concatenate(
                [jnp.where(cols == at + float(j), 1.0, 0.0).astype(BF16) for j in range(0, width, 128)],
                axis=1,
            )
        )
    return jnp.concatenate(made, axis=0)


def encode_kernel(parts, owner, node, grid, w1, bias, hidden, near, cross, code, owner_v, node_v, grid_v, w1_v, bias_v, one_hot, sems):
    small = [(owner, owner_v), (node, node_v), (w1, w1_v), (bias, bias_v)]
    copies = [pltpu.make_async_copy(a, b, sems.at[i]) for i, (a, b) in enumerate(small)]
    starts = range(0, grid.shape[0], ENCODE_BLOCK)
    blocks = [
        pltpu.make_async_copy(grid.at[pl.ds(r, ENCODE_BLOCK)], grid_v.at[pl.ds(r, ENCODE_BLOCK)], sems.at[4 + i])
        for i, r in enumerate(starts)
    ]
    for copy in copies + blocks[:1]:
        copy.start()
    copies[0].wait()
    copies[1].wait()
    for copy in blocks[1:]:
        copy.start()
    code[...] = slot_codes(owner_v[...], node_v[...], parts, near.shape[0])
    one_hot[...] = one_hot_down(code[...], 0, one_hot.shape[0])
    copies[2].wait()
    copies[3].wait()
    weights = w1_v[...] * 0.5
    offset = bias_v[...] * 0.5
    for r, copy in zip(starts, blocks):
        copy.wait()
        spot = slice(r, r + ENCODE_BLOCK)
        hidden[spot] = silu_of_twice(dot(grid_v[spot], weights) + offset).astype(BF16)
    rows = near.shape[0]
    cross[...] = dot(one_hot[rows:], hidden[...]).astype(BF16)
    near[...] = dot(one_hot[:rows], hidden[...]).astype(BF16)


def far_kernel(code, hidden, crossed, far):
    rows = far.shape[0]
    far[...] = (dot(one_hot_down(code[...], 4 * rows, rows), hidden[...]) + crossed[...].astype(F32)).astype(BF16)


def chip_kernel(after, code, hidden, halo_index, *refs):
    del after
    held, (own, sibling, pick, joined, kept, fetch), buffers, sems = refs[:5], refs[5:11], refs[11:16], refs[16]
    copies = [pltpu.make_async_copy(a, b, sems.at[i]) for i, (a, b) in enumerate(zip(held, buffers))]
    for copy in copies:
        copy.start()
    rows = own.shape[0]
    sibling[...] = dot(one_hot_down(code[...], 3 * rows, rows), hidden[...]).astype(BF16)
    own[...] = dot(one_hot_down(code[...], 2 * rows, rows), hidden[...])
    for r in range(0, fetch.shape[0], BLOCK):
        fetch[r : r + BLOCK] = one_hot_across(code[:, r : r + BLOCK], fetch.shape[1])
    for copy in copies:
        copy.wait()
    mesh, w2, w_src, w_out, w_mesh = buffers
    pairs = [(w2[...], w_src[0])] + [(w_out[i], w_src[i + 1]) for i in range(L - 1)] + [(w_out[L - 1], w_mesh[...])]
    for i, (first, second) in enumerate(pairs):
        joined[i] = (dot(first, second) * 0.5).astype(BF16)
    pick[...] = one_hot_down(halo_index[...], 0, rows)
    kept[...] = dot(picked(pick[...], mesh[...]), w_src[0]) * 0.5


def prepare_kernel(after, edges, pick, gather, gather_halo, lead, lead_halo):
    del after
    n, own = edges.shape[1], gather.shape[1]
    border = pick.shape[1]
    for k in range(edges.shape[0]):
        one_hot = one_hot_across(edges[k : k + 1, :], own + gather_halo.shape[1])
        gather[k * n : (k + 1) * n] = one_hot[:, :own]
        gather_halo[k * n : (k + 1) * n] = one_hot[:, own:]
        ahead = picked(pick[...], one_hot)
        lead[k * border : (k + 1) * border] = ahead[:, :own]
        lead_halo[k * border : (k + 1) * border] = ahead[:, own:]


def picked(pick, rows):
    return lax.dot_general(pick, rows, (((0,), (0,)), ((), ())), preferred_element_type=F32).astype(BF16)


def sums_kernel(after, own, sibling, near, far, pick, joined, kept, sums, halo):
    del after
    total = own[...] + sibling[...].astype(F32) + near[...].astype(F32) + far[...].astype(F32)
    sums[...] = total.astype(BF16)
    halo[...] = (kept[...] + dot(picked(pick[...], sums[...]), joined[0])).astype(BF16)


def latent_kernel(mesh, sums, w2, latent):
    latent[...] = (mesh[...].astype(F32) + dot(sums[...], w2[...])).astype(BF16)


def own_terms(layer, nodes, gather, source, w_dst, bias, before):
    n = nodes.shape[0]
    target = dot(nodes[...], w_dst[layer]) * 0.5 + bias[layer : layer + 1] * 0.5
    for k in range(gather.shape[0] // n):
        before[k * n : (k + 1) * n] = dot(gather[k * n : (k + 1) * n], source) + target


def project_kernel(layer, latent, w_src, w_dst, bias, gather, halo, w_next, *refs):
    source = (dot(latent[...], w_src[layer]) * 0.5).astype(BF16)
    if layer == L - 1:
        before, passed, kept = refs
        kept[...] = dot(latent[...], w_next[...]) * 0.5
    else:
        pick, lead, before, passed, kept, before_lead = refs
        nodes = picked(pick[...], latent[...])
        kept[...] = dot(nodes, w_next[layer + 1]) * 0.5
        own_terms(layer, nodes, lead, source, w_dst, bias, before_lead)
    passed[...] = halo[...]
    own_terms(layer, latent, gather, source, w_dst, bias, before)


def halo_table(across, beside):
    first = lax.axis_index("feat") == 0
    down = jnp.where(first, across[...], beside[...])
    up = jnp.where(first, beside[...], across[...])
    return jnp.concatenate([down, up], axis=0)


def edge_sums(n, before, gather_halo, table):
    total = None
    for k in range(before.shape[0] // n):
        spot = slice(k * n, (k + 1) * n)
        message = silu_of_twice(dot(gather_halo[spot], table) + before[spot])
        total = message if total is None else total + message
    return total.astype(BF16)


def lead_kernel(layer, before, across, beside, gather_halo, joined, kept, halo):
    sums = edge_sums(kept.shape[0], before, gather_halo, halo_table(across, beside))
    halo[...] = (kept[...] + dot(sums, joined[layer + 1])).astype(BF16)


def layer_kernel(layer, latent, before, across, beside, gather_halo, w_out, new):
    sums = edge_sums(latent.shape[0], before, gather_halo, halo_table(across, beside))
    new[...] = (latent[...].astype(F32) + dot(sums, w_out[layer])).astype(BF16)


def last_layer_kernel(before, across, beside, gather_halo, kept, joined, projected):
    sums = edge_sums(kept.shape[0], before, gather_halo, halo_table(across, beside))
    projected[...] = (kept[...] + dot(sums, joined[L])).astype(BF16)


def base_kernel(grid, w_grid, fetch, own, base, *pieces):
    rows = own.shape[0]
    cut_kernel(None, own, *pieces)
    for r in range(0, grid.shape[0], BLOCK):
        spot = slice(r, r + BLOCK)
        base[spot] = dot(grid[spot], w_grid[...]) * 0.5 + dot(fetch[spot, 2 * rows : 3 * rows], own[...])


def halve_kernel(first_after, after, own, left, right):
    del first_after, after
    half = left.shape[1]
    left[...] = own[:, :half]
    right[...] = own[:, half:]


def sibling_kernel(fetch, base, *refs):
    *pieces, out = refs
    table = jnp.concatenate([piece[...] for piece in pieces], axis=0)
    rows = table.shape[0]
    for r in range(0, base.shape[0], BLOCK):
        spot = slice(r, r + BLOCK)
        out[spot] = base[spot] + dot(fetch[spot, 3 * rows : 4 * rows], table)


def far_add_kernel(fetch, base, far, out):
    rows = far.shape[0]
    for r in range(0, base.shape[0], BLOCK):
        spot = slice(r, r + BLOCK)
        out[spot] = base[spot] + dot(fetch[spot, 4 * rows : 5 * rows], far[...])


def cross_add_kernel(fetch, base, *refs):
    *pieces, out = refs
    table = jnp.concatenate([piece[...] for piece in pieces], axis=0)
    rows = table.shape[0]
    for r in range(0, base.shape[0], BLOCK):
        spot = slice(r, r + BLOCK)
        out[spot] = base[spot] + dot(fetch[spot, rows : 2 * rows], table)


def cut_kernel(after, table, *pieces):
    del after
    row = column = 0
    for piece in pieces:
        rows, width = piece.shape
        piece[...] = table[row : row + rows, column : column + width]
        row += rows
        if row == table.shape[0]:
            row, column = 0, column + width


def pass_kernel(table, out):
    out[...] = table[...]


def ahead_of(block, starts, halved, finish):
    half = halved(0)
    for r in starts:
        ahead = halved(r + block) if r + block <= starts[-1] else None
        finish(r, silu_of_twice(half).astype(BF16))
        half = ahead


def decode_left_kernel(fetch, base, near, w_out, partial):
    rows, width = near.shape
    starts = range(0, base.shape[0], DECODE_BLOCK)

    def halved(r):
        spot = slice(r, r + DECODE_BLOCK)
        return base[spot, :width] + dot(fetch[spot, :rows], near[...])

    def finish(r, hidden):
        partial[r : r + DECODE_BLOCK] = dot(hidden, w_out[:width])

    ahead_of(DECODE_BLOCK, starts, halved, finish)


def decode_kernel(fetch, base, near, w_out, partial, out, out_v, sems):
    rows, width = near.shape
    starts = range(0, base.shape[0], DECODE_BLOCK)
    copies = []

    def halved(r):
        spot = slice(r, r + DECODE_BLOCK)
        return base[spot, width:] + dot(fetch[spot, :rows], near[...])

    def finish(r, hidden):
        spot = slice(r, r + DECODE_BLOCK)
        out_v[spot] = (partial[spot] + dot(hidden, w_out[width:])).astype(BF16)
        place = pl.ds(r, DECODE_BLOCK)
        copies.append(pltpu.make_async_copy(out_v.at[place], out.at[place], sems.at[len(copies)]))
        copies[-1].start()

    ahead_of(DECODE_BLOCK, starts, halved, finish)
    for copy in copies:
        copy.wait()


VM = pltpu.VMEM


def call(kernel, ins, outs, flops, scratch=(), vmem=24, spaces=None, out_space=VM):
    moved = sum(a.size * a.dtype.itemsize for a in ins)
    spaces = spaces or [VM] * len(ins)
    ins = [pltpu.with_memory_space_constraint(a, s) if s is pltpu.HBM else a for a, s in zip(ins, spaces)]
    return pl.pallas_call(
        kernel,
        in_specs=[pl.BlockSpec(memory_space=space) for space in spaces],
        out_specs=[pl.BlockSpec(memory_space=out_space) for _ in outs],
        out_shape=[jax.ShapeDtypeStruct(shape, dtype) for shape, dtype in outs],
        scratch_shapes=list(scratch),
        compiler_params=pltpu.CompilerParams(vmem_limit_bytes=vmem * MIB),
        cost_estimate=pl.CostEstimate(flops=flops, bytes_accessed=moved if flops > 1 else 1, transcendentals=0),
    )(*ins)


def body(
    grid,
    mesh_feat,
    owner,
    node,
    halo_index,
    edge_src,
    w_enc1,
    enc_bias,
    w_enc2,
    proc_src,
    proc_dst,
    proc_bias,
    proc_out,
    dec_grid,
    dec_mesh,
    dec_out,
):
    parts = lax.axis_size(AXES)
    rows, width = grid.shape
    mesh_rows = mesh_feat.shape[0]
    border = halo_index.shape[0]
    degree = edge_src.shape[1]
    part = functools.partial

    def sided(step):
        return [(i, (i + step) % parts if i % 2 == 0 else (i - step) % parts) for i in range(parts)]

    def swap(value):
        return lax.ppermute(value, AXES, sided(1))

    def to_across(value):
        return lax.ppermute(value, AXES, sided(-1))

    def to_near(value):
        return lax.ppermute(value, AXES, sided(-2))

    def to_far(value):
        return lax.ppermute(value, AXES, sided(2))

    table = ((mesh_rows, width), BF16)
    border_rows = ((border, width), BF16)
    unit = 2 * rows * width
    hidden, near, cross, code = call(
        part(encode_kernel, parts),
        [owner.reshape(1, rows), node.reshape(1, rows), grid, w_enc1, enc_bias.reshape(1, width)],
        [((rows, width), BF16), table, table, ((1, rows), jnp.int32)],
        unit * (width + 2 * mesh_rows),
        [
            VM((1, rows), jnp.int32),
            VM((1, rows), jnp.int32),
            VM((rows, width), BF16),
            VM((width, width), BF16),
            VM((1, width), F32),
            VM((2 * mesh_rows, rows), BF16),
            pltpu.SemaphoreType.DMA((4 + rows // ENCODE_BLOCK,)),
        ],
        spaces=[pltpu.HBM] * 5,
    )
    near = to_near(near)
    crossed = swap(cross)
    (sent,) = call(far_kernel, [code, hidden, crossed], [table], 1)
    far = to_far(sent)
    own, sibling, pick, joined, kept, fetch = call(
        chip_kernel,
        [sent, code, hidden, halo_index.reshape(1, border), mesh_feat, w_enc2, proc_src, proc_out, dec_mesh],
        [
            ((mesh_rows, width), F32),
            table,
            ((mesh_rows, border), BF16),
            ((L + 1, width, width), BF16),
            ((border, width), F32),
            ((rows, 5 * mesh_rows), BF16),
        ],
        unit * 2 * mesh_rows,
        [
            VM((mesh_rows, width), BF16),
            VM((width, width), BF16),
            VM((L, width, width), BF16),
            VM((L, width, width), BF16),
            VM((width, width), BF16),
            pltpu.SemaphoreType.DMA((5,)),
        ],
        spaces=[pl.ANY] + [VM] * 3 + [pltpu.HBM] * 5,
    )
    gather, gather_halo, lead, lead_halo = call(
        prepare_kernel,
        [near, edge_src.T, pick],
        [
            ((degree * mesh_rows, mesh_rows), BF16),
            ((degree * mesh_rows, 2 * border), BF16),
            ((degree * border, mesh_rows), BF16),
            ((degree * border, 2 * border), BF16),
        ],
        LONG,
        spaces=[pl.ANY, VM, VM],
    )
    sibling = swap(sibling)
    sums, halo = call(
        sums_kernel,
        [lead_halo, own, sibling, near, far, pick, joined, kept],
        [table, border_rows],
        2 * mesh_rows * width * width,
        spaces=[pl.ANY] + [VM] * 7,
    )
    across = to_across(halo)
    (latent,) = call(latent_kernel, [mesh_feat, sums, w_enc2], [table], 1)
    edge_terms = ((degree * mesh_rows, width), F32)
    for layer in range(L - 1):
        before, passed, kept, before_lead = call(
            part(project_kernel, layer),
            [latent, proc_src, proc_dst, proc_bias, gather, halo, proc_src, pick, lead],
            [edge_terms, border_rows, ((border, width), F32), ((degree * border, width), F32)],
            1,
        )
        beside = swap(passed)
        (across,) = call(pass_kernel, [across], [border_rows], LONG)
        (halo,) = call(
            part(lead_kernel, layer),
            [before_lead, across, beside, lead_halo, joined, kept],
            [border_rows],
            2 * border * width * (degree * 2 * border + 3 * width),
        )
        arrived = (across, beside)
        across = to_across(halo)
        (latent,) = call(
            part(layer_kernel, layer),
            [latent, before, *arrived, gather_halo, proc_out],
            [table],
            1,
        )
    before, passed, kept = call(
        part(project_kernel, L - 1),
        [latent, proc_src, proc_dst, proc_bias, gather, halo, dec_mesh],
        [edge_terms, border_rows, ((mesh_rows, width), F32)],
        1,
    )
    beside = swap(passed)
    (across,) = call(pass_kernel, [across], [border_rows], LONG)
    (projected,) = call(
        last_layer_kernel,
        [before, across, beside, gather_halo, kept, joined],
        [table],
        2 * mesh_rows * width * (degree * 2 * border + 2 * width),
    )
    far = to_near(projected)
    f32_rows = ((rows, width), F32)
    pieces = [((mesh_rows // 2, width), BF16)] * 2
    base, *passed = call(
        base_kernel,
        [grid, dec_grid, fetch, projected],
        [f32_rows, *pieces],
        1,
    )
    sibling = [swap(piece) for piece in passed]
    half = ((mesh_rows, width // 2), BF16)
    left, right = call(halve_kernel, [*sibling, projected], [half, half], 1, spaces=[pl.ANY, pl.ANY, VM])
    (base,) = call(sibling_kernel, [fetch, base, *sibling], [f32_rows], 1)
    left = to_far(left)
    right = to_far(right)
    shares = [((mesh_rows * share // 256, width), BF16) for share in (112, 80, 64)]
    passed = call(cut_kernel, [base, far], shares, 1, spaces=[pl.ANY, VM])
    cross = [swap(piece) for piece in passed]
    (base,) = call(far_add_kernel, [fetch, base, far], [f32_rows], 1)
    (base,) = call(cross_add_kernel, [fetch, base, *cross], [f32_rows], 1)
    (partial,) = call(decode_left_kernel, [fetch, base, left, dec_out], [f32_rows], 1)
    (out,) = call(
        decode_kernel,
        [fetch, base, right, dec_out, partial],
        [((rows, width), BF16)],
        unit * (width + mesh_rows),
        [VM((rows, width), BF16), pltpu.SemaphoreType.DMA((rows // DECODE_BLOCK,))],
        out_space=pltpu.HBM,
    )
    return out


def solution(mesh):
    rows = P(("group", "dom", "feat"), None)
    flat = P(("group", "dom", "feat"))
    return jax.shard_map(
        body,
        mesh=mesh,
        in_specs=(rows, rows, rows, flat, flat, rows) + (P(),) * 10,
        out_specs=rows,
        check_vma=False,
    )
```

```python
import functools

import jax
import jax.numpy as jnp
from jax import lax
from jax.experimental import pallas as pl
from jax.experimental.pallas import tpu as pltpu
from jax.sharding import PartitionSpec as P

L = 2
AXES = ("dom", "feat")
F32, BF16 = jnp.float32, jnp.bfloat16
MIB = 1 << 20
BLOCK = 512
ENCODE_BLOCK = 1024
DECODE_BLOCK = 256
LONG = 40_000_000_000


def silu_of_twice(half):
    return half + half * jnp.tanh(half)


def dot(a, b):
    return jnp.dot(a, b, preferred_element_type=F32)


def slot_codes(owner, node, parts, mesh_rows):
    core = lax.axis_index("feat")
    me = lax.axis_index("dom") * 2 + core
    slot = (owner - me) * (1 - 2 * core) + 2
    slot = jnp.where(slot < 0, slot + parts, slot)
    slot = jnp.where(slot >= parts, slot - parts, slot)
    return slot * mesh_rows + node


def one_hot_down(code, first, rows):
    at = lax.broadcasted_iota(jnp.int32, (rows, code.shape[1]), 0)
    return jnp.where(at == code - first, 1.0, 0.0).astype(BF16)


def one_hot_across(row, width):
    n = row.shape[1]
    row = row.astype(F32)
    made = []
    for i in range(0, n, 128):
        cols = jnp.broadcast_to(row[:, i : i + 128], (128, 128)).T
        at = lax.broadcasted_iota(jnp.int32, cols.shape, 1).astype(F32)
        made.append(
            jnp.concatenate(
                [jnp.where(cols == at + float(j), 1.0, 0.0).astype(BF16) for j in range(0, width, 128)],
                axis=1,
            )
        )
    return jnp.concatenate(made, axis=0)


def encode_kernel(parts, owner, node, grid, w1, bias, hidden, near, cross, code, owner_v, node_v, grid_v, w1_v, bias_v, one_hot, sems):
    small = [(owner, owner_v), (node, node_v), (w1, w1_v), (bias, bias_v)]
    copies = [pltpu.make_async_copy(a, b, sems.at[i]) for i, (a, b) in enumerate(small)]
    starts = range(0, grid.shape[0], ENCODE_BLOCK)
    blocks = [
        pltpu.make_async_copy(grid.at[pl.ds(r, ENCODE_BLOCK)], grid_v.at[pl.ds(r, ENCODE_BLOCK)], sems.at[4 + i])
        for i, r in enumerate(starts)
    ]
    for copy in copies + blocks[:1]:
        copy.start()
    copies[0].wait()
    copies[1].wait()
    for copy in blocks[1:]:
        copy.start()
    code[...] = slot_codes(owner_v[...], node_v[...], parts, near.shape[0])
    one_hot[...] = one_hot_down(code[...], 0, one_hot.shape[0])
    copies[2].wait()
    copies[3].wait()
    weights = w1_v[...] * 0.5
    offset = bias_v[...] * 0.5
    for r, copy in zip(starts, blocks):
        copy.wait()
        spot = slice(r, r + ENCODE_BLOCK)
        hidden[spot] = silu_of_twice(dot(grid_v[spot], weights) + offset).astype(BF16)
    rows = near.shape[0]
    cross[...] = dot(one_hot[rows:], hidden[...]).astype(BF16)
    near[...] = dot(one_hot[:rows], hidden[...]).astype(BF16)


def far_kernel(code, hidden, crossed, far):
    rows = far.shape[0]
    far[...] = (dot(one_hot_down(code[...], 4 * rows, rows), hidden[...]) + crossed[...].astype(F32)).astype(BF16)


def chip_kernel(after, code, hidden, halo_index, *refs):
    del after
    held, (own, sibling, pick, joined, kept, fetch), buffers, sems = refs[:5], refs[5:11], refs[11:16], refs[16]
    copies = [pltpu.make_async_copy(a, b, sems.at[i]) for i, (a, b) in enumerate(zip(held, buffers))]
    for copy in copies:
        copy.start()
    rows = own.shape[0]
    sibling[...] = dot(one_hot_down(code[...], 3 * rows, rows), hidden[...]).astype(BF16)
    own[...] = dot(one_hot_down(code[...], 2 * rows, rows), hidden[...])
    for r in range(0, fetch.shape[0], BLOCK):
        fetch[r : r + BLOCK] = one_hot_across(code[:, r : r + BLOCK], fetch.shape[1])
    for copy in copies:
        copy.wait()
    mesh, w2, w_src, w_out, w_mesh = buffers
    pairs = [(w2[...], w_src[0])] + [(w_out[i], w_src[i + 1]) for i in range(L - 1)] + [(w_out[L - 1], w_mesh[...])]
    for i, (first, second) in enumerate(pairs):
        joined[i] = (dot(first, second) * 0.5).astype(BF16)
    pick[...] = one_hot_down(halo_index[...], 0, rows)
    kept[...] = dot(picked(pick[...], mesh[...]), w_src[0]) * 0.5


def prepare_kernel(after, edges, pick, gather, gather_halo, lead, lead_halo):
    del after
    n, own = edges.shape[1], gather.shape[1]
    border = pick.shape[1]
    for k in range(edges.shape[0]):
        one_hot = one_hot_across(edges[k : k + 1, :], own + gather_halo.shape[1])
        gather[k * n : (k + 1) * n] = one_hot[:, :own]
        gather_halo[k * n : (k + 1) * n] = one_hot[:, own:]
        ahead = picked(pick[...], one_hot)
        lead[k * border : (k + 1) * border] = ahead[:, :own]
        lead_halo[k * border : (k + 1) * border] = ahead[:, own:]


def picked(pick, rows):
    return lax.dot_general(pick, rows, (((0,), (0,)), ((), ())), preferred_element_type=F32).astype(BF16)


def sums_kernel(after, own, sibling, near, far, pick, joined, kept, sums, halo):
    del after
    total = own[...] + sibling[...].astype(F32) + near[...].astype(F32) + far[...].astype(F32)
    sums[...] = total.astype(BF16)
    halo[...] = (kept[...] + dot(picked(pick[...], sums[...]), joined[0])).astype(BF16)


def latent_kernel(mesh, sums, w2, latent):
    latent[...] = (mesh[...].astype(F32) + dot(sums[...], w2[...])).astype(BF16)


def own_terms(layer, nodes, gather, source, w_dst, bias, before):
    n = nodes.shape[0]
    target = dot(nodes[...], w_dst[layer]) * 0.5 + bias[layer : layer + 1] * 0.5
    for k in range(gather.shape[0] // n):
        before[k * n : (k + 1) * n] = dot(gather[k * n : (k + 1) * n], source) + target


def project_kernel(layer, latent, w_src, w_dst, bias, gather, halo, w_next, *refs):
    source = (dot(latent[...], w_src[layer]) * 0.5).astype(BF16)
    if layer == L - 1:
        before, passed, kept = refs
        kept[...] = dot(latent[...], w_next[...]) * 0.5
    else:
        pick, lead, before, passed, kept, before_lead = refs
        nodes = picked(pick[...], latent[...])
        kept[...] = dot(nodes, w_next[layer + 1]) * 0.5
        own_terms(layer, nodes, lead, source, w_dst, bias, before_lead)
    passed[...] = halo[...]
    own_terms(layer, latent, gather, source, w_dst, bias, before)


def halo_table(across, beside):
    first = lax.axis_index("feat") == 0
    down = jnp.where(first, across[...], beside[...])
    up = jnp.where(first, beside[...], across[...])
    return jnp.concatenate([down, up], axis=0)


def edge_sums(n, before, gather_halo, table):
    total = None
    for k in range(before.shape[0] // n):
        spot = slice(k * n, (k + 1) * n)
        message = silu_of_twice(dot(gather_halo[spot], table) + before[spot])
        total = message if total is None else total + message
    return total.astype(BF16)


def lead_kernel(layer, before, across, beside, gather_halo, joined, kept, halo):
    sums = edge_sums(kept.shape[0], before, gather_halo, halo_table(across, beside))
    halo[...] = (kept[...] + dot(sums, joined[layer + 1])).astype(BF16)


def layer_kernel(layer, latent, before, across, beside, gather_halo, w_out, new):
    sums = edge_sums(latent.shape[0], before, gather_halo, halo_table(across, beside))
    new[...] = (latent[...].astype(F32) + dot(sums, w_out[layer])).astype(BF16)


def last_layer_kernel(before, across, beside, gather_halo, kept, joined, projected):
    sums = edge_sums(kept.shape[0], before, gather_halo, halo_table(across, beside))
    projected[...] = (kept[...] + dot(sums, joined[L])).astype(BF16)


def base_kernel(grid, w_grid, fetch, own, base, *pieces):
    rows = own.shape[0]
    cut_kernel(None, own, *pieces)
    for r in range(0, grid.shape[0], BLOCK):
        spot = slice(r, r + BLOCK)
        base[spot] = dot(grid[spot], w_grid[...]) * 0.5 + dot(fetch[spot, 2 * rows : 3 * rows], own[...])


def halve_kernel(first_after, after, own, left, right):
    del first_after, after
    half = left.shape[1]
    left[...] = own[:, :half]
    right[...] = own[:, half:]


def sibling_kernel(fetch, base, *refs):
    *pieces, out = refs
    table = jnp.concatenate([piece[...] for piece in pieces], axis=0)
    rows = table.shape[0]
    for r in range(0, base.shape[0], BLOCK):
        spot = slice(r, r + BLOCK)
        out[spot] = base[spot] + dot(fetch[spot, 3 * rows : 4 * rows], table)


def far_add_kernel(fetch, base, far, out):
    rows = far.shape[0]
    for r in range(0, base.shape[0], BLOCK):
        spot = slice(r, r + BLOCK)
        out[spot] = base[spot] + dot(fetch[spot, 4 * rows : 5 * rows], far[...])


def cross_add_kernel(fetch, base, *refs):
    *pieces, out = refs
    table = jnp.concatenate([piece[...] for piece in pieces], axis=0)
    rows = table.shape[0]
    for r in range(0, base.shape[0], BLOCK):
        spot = slice(r, r + BLOCK)
        out[spot] = base[spot] + dot(fetch[spot, rows : 2 * rows], table)


def cut_kernel(after, table, *pieces):
    del after
    row = column = 0
    for piece in pieces:
        rows, width = piece.shape
        piece[...] = table[row : row + rows, column : column + width]
        row += rows
        if row == table.shape[0]:
            row, column = 0, column + width


def pass_kernel(table, out):
    out[...] = table[...]


def ahead_of(block, starts, halved, finish):
    half = halved(0)
    for r in starts:
        ahead = halved(r + block) if r + block <= starts[-1] else None
        finish(r, silu_of_twice(half).astype(BF16))
        half = ahead


def decode_left_kernel(fetch, base, near, w_out, partial):
    rows, width = near.shape
    starts = range(0, base.shape[0], BLOCK)

    def halved(r):
        spot = slice(r, r + BLOCK)
        return base[spot, :width] + dot(fetch[spot, :rows], near[...])

    def finish(r, hidden):
        partial[r : r + BLOCK] = dot(hidden, w_out[:width])

    ahead_of(BLOCK, starts, halved, finish)


def decode_kernel(fetch, base, near, w_out, partial, out, out_v, sems):
    rows, width = near.shape
    starts = range(0, base.shape[0], DECODE_BLOCK)
    copies = []

    def halved(r):
        spot = slice(r, r + DECODE_BLOCK)
        return base[spot, width:] + dot(fetch[spot, :rows], near[...])

    def finish(r, hidden):
        spot = slice(r, r + DECODE_BLOCK)
        out_v[spot] = (partial[spot] + dot(hidden, w_out[width:])).astype(BF16)
        place = pl.ds(r, DECODE_BLOCK)
        copies.append(pltpu.make_async_copy(out_v.at[place], out.at[place], sems.at[len(copies)]))
        copies[-1].start()

    ahead_of(DECODE_BLOCK, starts, halved, finish)
    for copy in copies:
        copy.wait()


VM = pltpu.VMEM


def call(kernel, ins, outs, flops, scratch=(), vmem=24, spaces=None, out_space=VM):
    moved = sum(a.size * a.dtype.itemsize for a in ins)
    spaces = spaces or [VM] * len(ins)
    ins = [pltpu.with_memory_space_constraint(a, s) if s is pltpu.HBM else a for a, s in zip(ins, spaces)]
    return pl.pallas_call(
        kernel,
        in_specs=[pl.BlockSpec(memory_space=space) for space in spaces],
        out_specs=[pl.BlockSpec(memory_space=out_space) for _ in outs],
        out_shape=[jax.ShapeDtypeStruct(shape, dtype) for shape, dtype in outs],
        scratch_shapes=list(scratch),
        compiler_params=pltpu.CompilerParams(vmem_limit_bytes=vmem * MIB),
        cost_estimate=pl.CostEstimate(flops=flops, bytes_accessed=moved if flops > 1 else 1, transcendentals=0),
    )(*ins)


def body(
    grid,
    mesh_feat,
    owner,
    node,
    halo_index,
    edge_src,
    w_enc1,
    enc_bias,
    w_enc2,
    proc_src,
    proc_dst,
    proc_bias,
    proc_out,
    dec_grid,
    dec_mesh,
    dec_out,
):
    parts = lax.axis_size(AXES)
    rows, width = grid.shape
    mesh_rows = mesh_feat.shape[0]
    border = halo_index.shape[0]
    degree = edge_src.shape[1]
    part = functools.partial

    def sided(step):
        return [(i, (i + step) % parts if i % 2 == 0 else (i - step) % parts) for i in range(parts)]

    def swap(value):
        return lax.ppermute(value, AXES, sided(1))

    def to_across(value):
        return lax.ppermute(value, AXES, sided(-1))

    def to_near(value):
        return lax.ppermute(value, AXES, sided(-2))

    def to_far(value):
        return lax.ppermute(value, AXES, sided(2))

    table = ((mesh_rows, width), BF16)
    border_rows = ((border, width), BF16)
    unit = 2 * rows * width
    hidden, near, cross, code = call(
        part(encode_kernel, parts),
        [owner.reshape(1, rows), node.reshape(1, rows), grid, w_enc1, enc_bias.reshape(1, width)],
        [((rows, width), BF16), table, table, ((1, rows), jnp.int32)],
        unit * (width + 2 * mesh_rows),
        [
            VM((1, rows), jnp.int32),
            VM((1, rows), jnp.int32),
            VM((rows, width), BF16),
            VM((width, width), BF16),
            VM((1, width), F32),
            VM((2 * mesh_rows, rows), BF16),
            pltpu.SemaphoreType.DMA((4 + rows // ENCODE_BLOCK,)),
        ],
        spaces=[pltpu.HBM] * 5,
    )
    near = to_near(near)
    crossed = swap(cross)
    (sent,) = call(far_kernel, [code, hidden, crossed], [table], 1)
    far = to_far(sent)
    own, sibling, pick, joined, kept, fetch = call(
        chip_kernel,
        [sent, code, hidden, halo_index.reshape(1, border), mesh_feat, w_enc2, proc_src, proc_out, dec_mesh],
        [
            ((mesh_rows, width), F32),
            table,
            ((mesh_rows, border), BF16),
            ((L + 1, width, width), BF16),
            ((border, width), F32),
            ((rows, 5 * mesh_rows), BF16),
        ],
        unit * 2 * mesh_rows,
        [
            VM((mesh_rows, width), BF16),
            VM((width, width), BF16),
            VM((L, width, width), BF16),
            VM((L, width, width), BF16),
            VM((width, width), BF16),
            pltpu.SemaphoreType.DMA((5,)),
        ],
        spaces=[pl.ANY] + [VM] * 3 + [pltpu.HBM] * 5,
    )
    gather, gather_halo, lead, lead_halo = call(
        prepare_kernel,
        [near, edge_src.T, pick],
        [
            ((degree * mesh_rows, mesh_rows), BF16),
            ((degree * mesh_rows, 2 * border), BF16),
            ((degree * border, mesh_rows), BF16),
            ((degree * border, 2 * border), BF16),
        ],
        LONG,
        spaces=[pl.ANY, VM, VM],
    )
    sibling = swap(sibling)
    sums, halo = call(
        sums_kernel,
        [lead_halo, own, sibling, near, far, pick, joined, kept],
        [table, border_rows],
        2 * mesh_rows * width * width,
        spaces=[pl.ANY] + [VM] * 7,
    )
    across = to_across(halo)
    (latent,) = call(latent_kernel, [mesh_feat, sums, w_enc2], [table], 1)
    edge_terms = ((degree * mesh_rows, width), F32)
    for layer in range(L - 1):
        before, passed, kept, before_lead = call(
            part(project_kernel, layer),
            [latent, proc_src, proc_dst, proc_bias, gather, halo, proc_src, pick, lead],
            [edge_terms, border_rows, ((border, width), F32), ((degree * border, width), F32)],
            1,
        )
        beside = swap(passed)
        (across,) = call(pass_kernel, [across], [border_rows], LONG)
        (halo,) = call(
            part(lead_kernel, layer),
            [before_lead, across, beside, lead_halo, joined, kept],
            [border_rows],
            2 * border * width * (degree * 2 * border + 3 * width),
        )
        arrived = (across, beside)
        across = to_across(halo)
        (latent,) = call(
            part(layer_kernel, layer),
            [latent, before, *arrived, gather_halo, proc_out],
            [table],
            1,
        )
    before, passed, kept = call(
        part(project_kernel, L - 1),
        [latent, proc_src, proc_dst, proc_bias, gather, halo, dec_mesh],
        [edge_terms, border_rows, ((mesh_rows, width), F32)],
        1,
    )
    beside = swap(passed)
    (across,) = call(pass_kernel, [across], [border_rows], LONG)
    (projected,) = call(
        last_layer_kernel,
        [before, across, beside, gather_halo, kept, joined],
        [table],
        2 * mesh_rows * width * (degree * 2 * border + 2 * width),
    )
    far = to_near(projected)
    f32_rows = ((rows, width), F32)
    pieces = [((mesh_rows // 2, width), BF16)] * 2
    base, *passed = call(
        base_kernel,
        [grid, dec_grid, fetch, projected],
        [f32_rows, *pieces],
        1,
    )
    sibling = [swap(piece) for piece in passed]
    half = ((mesh_rows, width // 2), BF16)
    left, right = call(halve_kernel, [*sibling, projected], [half, half], 1, spaces=[pl.ANY, pl.ANY, VM])
    (base,) = call(sibling_kernel, [fetch, base, *sibling], [f32_rows], 1)
    left = to_far(left)
    right = to_far(right)
    shares = [((mesh_rows * share // 256, width), BF16) for share in (112, 80, 64)]
    passed = call(cut_kernel, [base, far], shares, 1, spaces=[pl.ANY, VM])
    cross = [swap(piece) for piece in passed]
    (base,) = call(far_add_kernel, [fetch, base, far], [f32_rows], 1)
    (base,) = call(cross_add_kernel, [fetch, base, *cross], [f32_rows], 1)
    (partial,) = call(decode_left_kernel, [fetch, base, left, dec_out], [f32_rows], 1)
    (out,) = call(
        decode_kernel,
        [fetch, base, right, dec_out, partial],
        [((rows, width), BF16)],
        unit * (width + mesh_rows),
        [VM((rows, width), BF16), pltpu.SemaphoreType.DMA((rows // DECODE_BLOCK,))],
        out_space=pltpu.HBM,
    )
    return out


def solution(mesh):
    rows = P(("group", "dom", "feat"), None)
    flat = P(("group", "dom", "feat"))
    return jax.shard_map(
        body,
        mesh=mesh,
        in_specs=(rows, rows, rows, flat, flat, rows) + (P(),) * 10,
        out_specs=rows,
        check_vma=False,
    )
```

```python
import functools

import jax
import jax.numpy as jnp
from jax import lax
from jax.experimental import pallas as pl
from jax.experimental.pallas import tpu as pltpu
from jax.sharding import PartitionSpec as P

L = 2
AXES = ("dom", "feat")
F32, BF16 = jnp.float32, jnp.bfloat16
MIB = 1 << 20
BLOCK = 512
ENCODE_BLOCK = 1024
ENCODE_STEP = 512
DECODE_BLOCK = 256
LONG = 40_000_000_000


def silu_of_twice(half):
    return half + half * jnp.tanh(half)


def dot(a, b):
    return jnp.dot(a, b, preferred_element_type=F32)


def slot_codes(owner, node, parts, mesh_rows):
    core = lax.axis_index("feat")
    me = lax.axis_index("dom") * 2 + core
    slot = (owner - me) * (1 - 2 * core) + 2
    slot = jnp.where(slot < 0, slot + parts, slot)
    slot = jnp.where(slot >= parts, slot - parts, slot)
    return slot * mesh_rows + node


def one_hot_down(code, first, rows):
    at = lax.broadcasted_iota(jnp.int32, (rows, code.shape[1]), 0)
    return jnp.where(at == code - first, 1.0, 0.0).astype(BF16)


def one_hot_across(row, width):
    n = row.shape[1]
    row = row.astype(F32)
    made = []
    for i in range(0, n, 128):
        cols = jnp.broadcast_to(row[:, i : i + 128], (128, 128)).T
        at = lax.broadcasted_iota(jnp.int32, cols.shape, 1).astype(F32)
        made.append(
            jnp.concatenate(
                [jnp.where(cols == at + float(j), 1.0, 0.0).astype(BF16) for j in range(0, width, 128)],
                axis=1,
            )
        )
    return jnp.concatenate(made, axis=0)


def encode_kernel(parts, owner, node, grid, w1, bias, hidden, near, cross, code, owner_v, node_v, grid_v, w1_v, bias_v, one_hot, sems):
    small = [(owner, owner_v), (node, node_v), (w1, w1_v), (bias, bias_v)]
    copies = [pltpu.make_async_copy(a, b, sems.at[i]) for i, (a, b) in enumerate(small)]
    starts = range(0, grid.shape[0], ENCODE_BLOCK)
    blocks = [
        pltpu.make_async_copy(grid.at[pl.ds(r, ENCODE_BLOCK)], grid_v.at[pl.ds(r, ENCODE_BLOCK)], sems.at[4 + i])
        for i, r in enumerate(starts)
    ]
    for copy in copies + blocks[:1]:
        copy.start()
    copies[0].wait()
    copies[1].wait()
    for copy in blocks[1:]:
        copy.start()
    code[...] = slot_codes(owner_v[...], node_v[...], parts, near.shape[0])
    one_hot[...] = one_hot_down(code[...], 0, one_hot.shape[0])
    copies[2].wait()
    copies[3].wait()
    weights = w1_v[...] * 0.5
    offset = bias_v[...] * 0.5
    def halved(r):
        if r % ENCODE_BLOCK == 0:
            blocks[r // ENCODE_BLOCK].wait()
        return dot(grid_v[r : r + ENCODE_STEP], weights) + offset

    half = halved(0)
    for r in range(0, grid.shape[0], ENCODE_STEP):
        ahead = halved(r + ENCODE_STEP) if r + ENCODE_STEP < grid.shape[0] else None
        hidden[r : r + ENCODE_STEP] = silu_of_twice(half).astype(BF16)
        half = ahead
    rows = near.shape[0]
    cross[...] = dot(one_hot[rows:], hidden[...]).astype(BF16)
    near[...] = dot(one_hot[:rows], hidden[...]).astype(BF16)


def far_kernel(code, hidden, crossed, far):
    rows = far.shape[0]
    far[...] = (dot(one_hot_down(code[...], 4 * rows, rows), hidden[...]) + crossed[...].astype(F32)).astype(BF16)


def chip_kernel(after, code, hidden, halo_index, *refs):
    del after
    held, (own, sibling, pick, joined, kept, fetch), buffers, sems = refs[:5], refs[5:11], refs[11:16], refs[16]
    copies = [pltpu.make_async_copy(a, b, sems.at[i]) for i, (a, b) in enumerate(zip(held, buffers))]
    for copy in copies:
        copy.start()
    rows = own.shape[0]
    sibling[...] = dot(one_hot_down(code[...], 3 * rows, rows), hidden[...]).astype(BF16)
    own[...] = dot(one_hot_down(code[...], 2 * rows, rows), hidden[...])
    for r in range(0, fetch.shape[0], BLOCK):
        fetch[r : r + BLOCK] = one_hot_across(code[:, r : r + BLOCK], fetch.shape[1])
    for copy in copies:
        copy.wait()
    mesh, w2, w_src, w_out, w_mesh = buffers
    pairs = [(w2[...], w_src[0])] + [(w_out[i], w_src[i + 1]) for i in range(L - 1)] + [(w_out[L - 1], w_mesh[...])]
    for i, (first, second) in enumerate(pairs):
        joined[i] = (dot(first, second) * 0.5).astype(BF16)
    pick[...] = one_hot_down(halo_index[...], 0, rows)
    kept[...] = dot(picked(pick[...], mesh[...]), w_src[0]) * 0.5


def prepare_kernel(after, edges, pick, gather, gather_halo, lead, lead_halo):
    del after
    n, own = edges.shape[1], gather.shape[1]
    border = pick.shape[1]
    for k in range(edges.shape[0]):
        one_hot = one_hot_across(edges[k : k + 1, :], own + gather_halo.shape[1])
        gather[k * n : (k + 1) * n] = one_hot[:, :own]
        gather_halo[k * n : (k + 1) * n] = one_hot[:, own:]
        ahead = picked(pick[...], one_hot)
        lead[k * border : (k + 1) * border] = ahead[:, :own]
        lead_halo[k * border : (k + 1) * border] = ahead[:, own:]


def picked(pick, rows):
    return lax.dot_general(pick, rows, (((0,), (0,)), ((), ())), preferred_element_type=F32).astype(BF16)


def sums_kernel(after, own, sibling, near, far, pick, joined, kept, sums, halo):
    del after
    total = own[...] + sibling[...].astype(F32) + near[...].astype(F32) + far[...].astype(F32)
    sums[...] = total.astype(BF16)
    halo[...] = (kept[...] + dot(picked(pick[...], sums[...]), joined[0])).astype(BF16)


def latent_kernel(mesh, sums, w2, latent):
    latent[...] = (mesh[...].astype(F32) + dot(sums[...], w2[...])).astype(BF16)


def own_terms(layer, nodes, gather, source, w_dst, bias, before):
    n = nodes.shape[0]
    target = dot(nodes[...], w_dst[layer]) * 0.5 + bias[layer : layer + 1] * 0.5
    for k in range(gather.shape[0] // n):
        before[k * n : (k + 1) * n] = dot(gather[k * n : (k + 1) * n], source) + target


def project_kernel(layer, latent, w_src, w_dst, bias, gather, halo, w_next, *refs):
    source = (dot(latent[...], w_src[layer]) * 0.5).astype(BF16)
    if layer == L - 1:
        before, passed, kept = refs
        kept[...] = dot(latent[...], w_next[...]) * 0.5
    else:
        pick, lead, before, passed, kept, before_lead = refs
        nodes = picked(pick[...], latent[...])
        kept[...] = dot(nodes, w_next[layer + 1]) * 0.5
        own_terms(layer, nodes, lead, source, w_dst, bias, before_lead)
    passed[...] = halo[...]
    own_terms(layer, latent, gather, source, w_dst, bias, before)


def halo_table(across, beside):
    first = lax.axis_index("feat") == 0
    down = jnp.where(first, across[...], beside[...])
    up = jnp.where(first, beside[...], across[...])
    return jnp.concatenate([down, up], axis=0)


def edge_sums(n, before, gather_halo, table):
    total = None
    for k in range(before.shape[0] // n):
        spot = slice(k * n, (k + 1) * n)
        message = silu_of_twice(dot(gather_halo[spot], table) + before[spot])
        total = message if total is None else total + message
    return total.astype(BF16)


def lead_kernel(layer, before, across, beside, gather_halo, joined, kept, halo):
    sums = edge_sums(kept.shape[0], before, gather_halo, halo_table(across, beside))
    halo[...] = (kept[...] + dot(sums, joined[layer + 1])).astype(BF16)


def layer_kernel(layer, latent, before, across, beside, gather_halo, w_out, new):
    sums = edge_sums(latent.shape[0], before, gather_halo, halo_table(across, beside))
    new[...] = (latent[...].astype(F32) + dot(sums, w_out[layer])).astype(BF16)


def last_layer_kernel(before, across, beside, gather_halo, kept, joined, projected):
    sums = edge_sums(kept.shape[0], before, gather_halo, halo_table(across, beside))
    projected[...] = (kept[...] + dot(sums, joined[L])).astype(BF16)


def base_kernel(grid, w_grid, fetch, own, base, *pieces):
    rows = own.shape[0]
    cut_kernel(None, own, *pieces)
    for r in range(0, grid.shape[0], BLOCK):
        spot = slice(r, r + BLOCK)
        base[spot] = dot(grid[spot], w_grid[...]) * 0.5 + dot(fetch[spot, 2 * rows : 3 * rows], own[...])


def halve_kernel(first_after, after, own, left, right):
    del first_after, after
    half = left.shape[1]
    left[...] = own[:, :half]
    right[...] = own[:, half:]


def sibling_kernel(fetch, base, *refs):
    *pieces, out = refs
    table = jnp.concatenate([piece[...] for piece in pieces], axis=0)
    rows = table.shape[0]
    for r in range(0, base.shape[0], BLOCK):
        spot = slice(r, r + BLOCK)
        out[spot] = base[spot] + dot(fetch[spot, 3 * rows : 4 * rows], table)


def far_add_kernel(fetch, base, far, out):
    rows = far.shape[0]
    for r in range(0, base.shape[0], BLOCK):
        spot = slice(r, r + BLOCK)
        out[spot] = base[spot] + dot(fetch[spot, 4 * rows : 5 * rows], far[...])


def cross_add_kernel(fetch, base, *refs):
    *pieces, out = refs
    table = jnp.concatenate([piece[...] for piece in pieces], axis=0)
    rows = table.shape[0]
    for r in range(0, base.shape[0], BLOCK):
        spot = slice(r, r + BLOCK)
        out[spot] = base[spot] + dot(fetch[spot, rows : 2 * rows], table)


def cut_kernel(after, table, *pieces):
    del after
    row = column = 0
    for piece in pieces:
        rows, width = piece.shape
        piece[...] = table[row : row + rows, column : column + width]
        row += rows
        if row == table.shape[0]:
            row, column = 0, column + width


def pass_kernel(table, out):
    out[...] = table[...]


def ahead_of(block, starts, halved, finish):
    half = halved(0)
    for r in starts:
        ahead = halved(r + block) if r + block <= starts[-1] else None
        finish(r, silu_of_twice(half).astype(BF16))
        half = ahead


def decode_left_kernel(fetch, base, near, w_out, partial):
    rows, width = near.shape
    starts = range(0, base.shape[0], BLOCK)

    def halved(r):
        spot = slice(r, r + BLOCK)
        return base[spot, :width] + dot(fetch[spot, :rows], near[...])

    def finish(r, hidden):
        partial[r : r + BLOCK] = dot(hidden, w_out[:width])

    ahead_of(BLOCK, starts, halved, finish)


def decode_kernel(fetch, base, near, w_out, partial, out, out_v, sems):
    rows, width = near.shape
    starts = range(0, base.shape[0], DECODE_BLOCK)
    copies = []

    def halved(r):
        spot = slice(r, r + DECODE_BLOCK)
        return base[spot, width:] + dot(fetch[spot, :rows], near[...])

    def finish(r, hidden):
        spot = slice(r, r + DECODE_BLOCK)
        out_v[spot] = (partial[spot] + dot(hidden, w_out[width:])).astype(BF16)
        place = pl.ds(r, DECODE_BLOCK)
        copies.append(pltpu.make_async_copy(out_v.at[place], out.at[place], sems.at[len(copies)]))
        copies[-1].start()

    ahead_of(DECODE_BLOCK, starts, halved, finish)
    for copy in copies:
        copy.wait()


VM = pltpu.VMEM


def call(kernel, ins, outs, flops, scratch=(), vmem=24, spaces=None, out_space=VM):
    moved = sum(a.size * a.dtype.itemsize for a in ins)
    spaces = spaces or [VM] * len(ins)
    ins = [pltpu.with_memory_space_constraint(a, s) if s is pltpu.HBM else a for a, s in zip(ins, spaces)]
    return pl.pallas_call(
        kernel,
        in_specs=[pl.BlockSpec(memory_space=space) for space in spaces],
        out_specs=[pl.BlockSpec(memory_space=out_space) for _ in outs],
        out_shape=[jax.ShapeDtypeStruct(shape, dtype) for shape, dtype in outs],
        scratch_shapes=list(scratch),
        compiler_params=pltpu.CompilerParams(vmem_limit_bytes=vmem * MIB),
        cost_estimate=pl.CostEstimate(flops=flops, bytes_accessed=moved if flops > 1 else 1, transcendentals=0),
    )(*ins)


def body(
    grid,
    mesh_feat,
    owner,
    node,
    halo_index,
    edge_src,
    w_enc1,
    enc_bias,
    w_enc2,
    proc_src,
    proc_dst,
    proc_bias,
    proc_out,
    dec_grid,
    dec_mesh,
    dec_out,
):
    parts = lax.axis_size(AXES)
    rows, width = grid.shape
    mesh_rows = mesh_feat.shape[0]
    border = halo_index.shape[0]
    degree = edge_src.shape[1]
    part = functools.partial

    def sided(step):
        return [(i, (i + step) % parts if i % 2 == 0 else (i - step) % parts) for i in range(parts)]

    def swap(value):
        return lax.ppermute(value, AXES, sided(1))

    def to_across(value):
        return lax.ppermute(value, AXES, sided(-1))

    def to_near(value):
        return lax.ppermute(value, AXES, sided(-2))

    def to_far(value):
        return lax.ppermute(value, AXES, sided(2))

    table = ((mesh_rows, width), BF16)
    border_rows = ((border, width), BF16)
    unit = 2 * rows * width
    hidden, near, cross, code = call(
        part(encode_kernel, parts),
        [owner.reshape(1, rows), node.reshape(1, rows), grid, w_enc1, enc_bias.reshape(1, width)],
        [((rows, width), BF16), table, table, ((1, rows), jnp.int32)],
        unit * (width + 2 * mesh_rows),
        [
            VM((1, rows), jnp.int32),
            VM((1, rows), jnp.int32),
            VM((rows, width), BF16),
            VM((width, width), BF16),
            VM((1, width), F32),
            VM((2 * mesh_rows, rows), BF16),
            pltpu.SemaphoreType.DMA((4 + rows // ENCODE_BLOCK,)),
        ],
        spaces=[pltpu.HBM] * 5,
    )
    near = to_near(near)
    crossed = swap(cross)
    (sent,) = call(far_kernel, [code, hidden, crossed], [table], 1)
    far = to_far(sent)
    own, sibling, pick, joined, kept, fetch = call(
        chip_kernel,
        [sent, code, hidden, halo_index.reshape(1, border), mesh_feat, w_enc2, proc_src, proc_out, dec_mesh],
        [
            ((mesh_rows, width), F32),
            table,
            ((mesh_rows, border), BF16),
            ((L + 1, width, width), BF16),
            ((border, width), F32),
            ((rows, 5 * mesh_rows), BF16),
        ],
        unit * 2 * mesh_rows,
        [
            VM((mesh_rows, width), BF16),
            VM((width, width), BF16),
            VM((L, width, width), BF16),
            VM((L, width, width), BF16),
            VM((width, width), BF16),
            pltpu.SemaphoreType.DMA((5,)),
        ],
        spaces=[pl.ANY] + [VM] * 3 + [pltpu.HBM] * 5,
    )
    gather, gather_halo, lead, lead_halo = call(
        prepare_kernel,
        [near, edge_src.T, pick],
        [
            ((degree * mesh_rows, mesh_rows), BF16),
            ((degree * mesh_rows, 2 * border), BF16),
            ((degree * border, mesh_rows), BF16),
            ((degree * border, 2 * border), BF16),
        ],
        LONG,
        spaces=[pl.ANY, VM, VM],
    )
    sibling = swap(sibling)
    sums, halo = call(
        sums_kernel,
        [lead_halo, own, sibling, near, far, pick, joined, kept],
        [table, border_rows],
        2 * mesh_rows * width * width,
        spaces=[pl.ANY] + [VM] * 7,
    )
    across = to_across(halo)
    (latent,) = call(latent_kernel, [mesh_feat, sums, w_enc2], [table], 1)
    edge_terms = ((degree * mesh_rows, width), F32)
    for layer in range(L - 1):
        before, passed, kept, before_lead = call(
            part(project_kernel, layer),
            [latent, proc_src, proc_dst, proc_bias, gather, halo, proc_src, pick, lead],
            [edge_terms, border_rows, ((border, width), F32), ((degree * border, width), F32)],
            1,
        )
        beside = swap(passed)
        (across,) = call(pass_kernel, [across], [border_rows], LONG)
        (halo,) = call(
            part(lead_kernel, layer),
            [before_lead, across, beside, lead_halo, joined, kept],
            [border_rows],
            2 * border * width * (degree * 2 * border + 3 * width),
        )
        arrived = (across, beside)
        across = to_across(halo)
        (latent,) = call(
            part(layer_kernel, layer),
            [latent, before, *arrived, gather_halo, proc_out],
            [table],
            1,
        )
    before, passed, kept = call(
        part(project_kernel, L - 1),
        [latent, proc_src, proc_dst, proc_bias, gather, halo, dec_mesh],
        [edge_terms, border_rows, ((mesh_rows, width), F32)],
        1,
    )
    beside = swap(passed)
    (across,) = call(pass_kernel, [across], [border_rows], LONG)
    (projected,) = call(
        last_layer_kernel,
        [before, across, beside, gather_halo, kept, joined],
        [table],
        2 * mesh_rows * width * (degree * 2 * border + 2 * width),
    )
    far = to_near(projected)
    f32_rows = ((rows, width), F32)
    pieces = [((mesh_rows // 2, width), BF16)] * 2
    base, *passed = call(
        base_kernel,
        [grid, dec_grid, fetch, projected],
        [f32_rows, *pieces],
        1,
    )
    sibling = [swap(piece) for piece in passed]
    half = ((mesh_rows, width // 2), BF16)
    left, right = call(halve_kernel, [*sibling, projected], [half, half], 1, spaces=[pl.ANY, pl.ANY, VM])
    (base,) = call(sibling_kernel, [fetch, base, *sibling], [f32_rows], 1)
    left = to_far(left)
    right = to_far(right)
    shares = [((mesh_rows * share // 256, width), BF16) for share in (112, 80, 64)]
    passed = call(cut_kernel, [base, far], shares, 1, spaces=[pl.ANY, VM])
    cross = [swap(piece) for piece in passed]
    (base,) = call(far_add_kernel, [fetch, base, far], [f32_rows], 1)
    (base,) = call(cross_add_kernel, [fetch, base, *cross], [f32_rows], 1)
    (partial,) = call(decode_left_kernel, [fetch, base, left, dec_out], [f32_rows], 1)
    (out,) = call(
        decode_kernel,
        [fetch, base, right, dec_out, partial],
        [((rows, width), BF16)],
        unit * (width + mesh_rows),
        [VM((rows, width), BF16), pltpu.SemaphoreType.DMA((rows // DECODE_BLOCK,))],
        out_space=pltpu.HBM,
    )
    return out


def solution(mesh):
    rows = P(("group", "dom", "feat"), None)
    flat = P(("group", "dom", "feat"))
    return jax.shard_map(
        body,
        mesh=mesh,
        in_specs=(rows, rows, rows, flat, flat, rows) + (P(),) * 10,
        out_specs=rows,
        check_vma=False,
    )
```
